512 devices in a mesh: row: 16 (over x, y), col: 32 (over z, core).
Axes of the slice: x: 4, y: 4, z: 16, core: 2. Of those that a mesh axis runs over, the one named last changes fastest.
Arguments:
- features: bfloat16 [65536, 256], P(('col', 'row')), may hold values from -6 to 6
- weight: bfloat16 [256, 256], replicated, may hold values from -0.375 to 0.375
- tile_values: bfloat16 [16, 32, 32, 128, 128], P('row', 'col'), may hold values from -0.125 to 0.125
- tile_rows: int32 [16, 32, 32], P('row', 'col'), may hold values from 0 to 31, as said below
- tile_cols: int32 [16, 32, 32], P('row', 'col'), may hold values from 0 to 15, as said below
- tile_count: int32 [16, 32], P('row', 'col'), may hold values from 4 to 32, as said below
- cotangent: bfloat16 [65536, 256], P(('row', 'col')), may hold values from -6 to 6
Outputs:
- output: bfloat16 [65536, 256], P(('row', 'col'))
- feature_grad: bfloat16 [65536, 256], P(('col', 'row'))
- weight_grad: float32 [256, 256], replicated
The draws below stay inside these ranges and needn't reach their ends.
Inputs may be any that keep to these rules, and one draw needn't show every extreme that they name: `tile_rows`: slots of one device name distinct tiles; slots at or beyond tile_count are unused. `tile_cols`: slots of one device name distinct tiles; slots at or beyond tile_count are unused. `tile_count`: some device uses all 32 slots.
All inputs are finite; a program needn't handle non-finite values.
Results may differ from the reference program's by a relative error of at most 0.025.
Values may be sent and summed in bfloat16 or wider, within the bound.
A program may use at most 64 MiB of HBM per device.

```python
import math
import jax
import jax.numpy as jnp
from jax import lax

F = 256
TILE = 128
NODES = 65536
ROW_TILES = 32
COL_TILES = 16
KT = 32
N_ROW = 16
N_COL = 32


def tile_slots(key):
    slot_total = ROW_TILES * COL_TILES
    scores = jax.random.randint(key, (N_ROW, N_COL, slot_total), 0, 65536)
    scores = scores * slot_total + jnp.arange(slot_total, dtype=jnp.int32)
    ordered = jnp.argsort(-scores, axis=-1, stable=True)[..., :KT]
    return ordered.astype(jnp.int32)


def draw_tile_rows(key, part):
    chosen = tile_slots(key)
    return chosen // COL_TILES


def draw_tile_cols(key, part):
    chosen = tile_slots(key)
    return chosen % COL_TILES


def draw_tile_count(key, part):
    key = jax.random.fold_in(key, 3)
    level_key, pick_key = jax.random.split(key)
    levels = jax.random.randint(level_key, (N_ROW * N_COL,), 0, 4)
    counts = KT // jnp.left_shift(jnp.int32(1), levels)
    fullest = jax.random.randint(pick_key, (), 0, N_ROW * N_COL)
    counts = jnp.where(jnp.arange(N_ROW * N_COL, dtype=jnp.int32) == fullest, KT, counts)
    return counts.reshape(N_ROW, N_COL).astype(jnp.int32)


def block_levels(stream_key, extent, cuts, least, top_value):
    gain = 1.0
    for dim, blocks in cuts:
        draws = jax.random.uniform(jax.random.fold_in(jax.random.fold_in(stream_key, 6), dim), (blocks,), jnp.float32, least / len(cuts), top_value / len(cuts))
        gain = gain * jnp.repeat(jnp.exp(draws), extent[dim] // blocks).reshape((-1,) + (1,) * (len(extent) - 1 - dim))
    return gain


def gaussian(rng, shape, width, reach, shards=(), held_as=jnp.bfloat16):
    loudness = block_levels(rng, shape, shards, -0.22, 0.18) if shards else 1.0
    array = jax.random.normal(rng, shape, jnp.float32) * width * loudness
    return jnp.minimum(jnp.maximum(array, -reach), reach).astype(held_as)


def setup_inputs(seed: int = 0) -> dict:
    arg_keys = jax.random.split(jax.random.key(seed), 8)
    features = gaussian(arg_keys[0], (NODES, F), 1.0, 6.0, ((0, 512),))
    weight = gaussian(arg_keys[1], (F, F), F ** -0.5, 0.375)
    tile_values = gaussian(arg_keys[2], (N_ROW, N_COL, KT, TILE, TILE), (KT * TILE // 2) ** -0.5, 0.125, ((0, 16), (1, 32)))
    tile_rows = draw_tile_rows(jax.random.fold_in(arg_keys[7], 71), 0)
    tile_cols = draw_tile_cols(jax.random.fold_in(arg_keys[7], 71), 0)
    tile_count = draw_tile_count(jax.random.fold_in(arg_keys[7], 71), 0)
    cotangent = gaussian(arg_keys[6], (NODES, F), 1.0, 6.0, ((0, 512),))
    return {"features": features, "weight": weight, "tile_values": tile_values, "tile_rows": tile_rows, "tile_cols": tile_cols, "tile_count": tile_count, "cotangent": cotangent}


def rounded(values):
    return lax.optimization_barrier(values.astype(jnp.bfloat16)).astype(jnp.float32)

def tile_terms(values, source, target, tile_total, panel_tiles, out_tiles, transposed):
    picked = panel_tiles[source]
    form = 'kji,kjf->kif' if transposed else 'kij,kjf->kif'
    products = jnp.einsum(form, values.astype(jnp.float32), picked.astype(jnp.float32))
    active = (jnp.arange(values.shape[0], dtype=jnp.int32) < tile_total).astype(jnp.float32)
    products = products * active[:, None, None]
    empty = jnp.zeros((out_tiles, products.shape[1], products.shape[2]), jnp.float32)
    return empty.at[target].add(products)

def reference(features, weight, tile_values, tile_rows, tile_cols, tile_count, cotangent):
    feature_tiles = features.reshape(N_COL, COL_TILES, TILE, F)

    def forward_block(row_index):

        def advance(total, col_index):
            term = tile_terms(tile_values[row_index, col_index], tile_cols[row_index, col_index], tile_rows[row_index, col_index], tile_count[row_index, col_index], feature_tiles[col_index], ROW_TILES, False)
            return (total + rounded(term), None)
        total, _ = lax.scan(advance, jnp.zeros((ROW_TILES, TILE, F), jnp.float32), jnp.arange(N_COL, dtype=jnp.int32))
        return total
    aggregated = lax.map(forward_block, jnp.arange(N_ROW, dtype=jnp.int32)).reshape(NODES, F).astype(jnp.bfloat16)
    preact = jnp.dot(aggregated, weight, preferred_element_type=jnp.float32)
    logistic = jax.nn.sigmoid(preact)
    output = (preact * logistic).astype(jnp.bfloat16)
    pre_grad = (cotangent.astype(jnp.float32) * logistic * (1.0 + preact * (1.0 - logistic))).astype(jnp.bfloat16)
    weight_grad = jnp.dot(aggregated.T, pre_grad, preferred_element_type=jnp.float32) * (1.0 / math.sqrt(NODES))
    aggregate_grad = jnp.dot(pre_grad, weight.T, preferred_element_type=jnp.float32).astype(jnp.bfloat16)
    grad_tiles = aggregate_grad.reshape(N_ROW, ROW_TILES, TILE, F)

    def backward_block(col_index):

        def advance(total, row_index):
            term = tile_terms(tile_values[row_index, col_index], tile_rows[row_index, col_index], tile_cols[row_index, col_index], tile_count[row_index, col_index], grad_tiles[row_index], COL_TILES, True)
            return (total + rounded(term), None)
        total, _ = lax.scan(advance, jnp.zeros((COL_TILES, TILE, F), jnp.float32), jnp.arange(N_ROW, dtype=jnp.int32))
        return total
    feature_grad = lax.map(backward_block, jnp.arange(N_COL, dtype=jnp.int32)).reshape(NODES, F).astype(jnp.bfloat16)
    return (output, feature_grad, weight_grad)
```

```python
import functools
import math

import jax
import jax.numpy as jnp
from jax import lax
from jax.experimental import pallas as pl
from jax.experimental.pallas import tpu as pltpu
from jax.sharding import PartitionSpec as P

MESH = pl.DeviceIdType.MESH
BF = jnp.bfloat16
F32 = jnp.float32
NX, NY, NZ, NR = 4, 4, 16, 16
SLOTS, ROW_T, COL_T, T = 32, 32, 16, 128
H = 128


def remote(src, dst, send, recv, device):
    return pltpu.make_async_remote_copy(
        src_ref=src, dst_ref=dst, send_sem=send, recv_sem=recv, device_id=device, device_id_type=MESH
    )


def slot_tables(rows, cols, count, table):
    sub = lax.broadcasted_iota(jnp.int32, (SLOTS, SLOTS), 0)
    lane = lax.broadcasted_iota(jnp.int32, (SLOTS, SLOTS), 1)
    used = sub < count[...]

    def latest(mask):
        found = jnp.max(jnp.where(mask, sub, -1), axis=0, keepdims=True)
        return jnp.where(found < 0, SLOTS, found)

    for base, ref in ((0, rows), (2, cols)):
        along = jnp.broadcast_to(ref[...], (SLOTS, SLOTS))
        down = jnp.sum(jnp.where(sub == lane, along, 0), axis=1, keepdims=True)
        table[base : base + 1, :SLOTS] = latest((down == along) & (sub < lane) & used)
        table[base + 1 : base + 2, :SLOTS] = latest((down == lane) & used)
        table[4 + base // 2 : 5 + base // 2, :SLOTS] = ref[...]


def kernel(
    feat, weight, vals, rows, cols, count, cot, out, fgrad, wgrad,
    table, idx, panel, acc, pair_out, pair_in, own_out, own_in, first, chain, side_in,
    grads, back_out, back_in, w_loc, w_pair, w_sum, w_x, w_z, w_all, w_other,
    idx_sem, g_send, g_recv, p_send, p_recv, o_send, o_recv, c_send, c_recv, f_send, f_recv,
    a_send, a_recv, q_send, q_recv, b_send, b_recv, wp_send, wp_recv, wx_send, wx_recv,
    wz_send, wz_recv, wa_send, wa_recv, wo_send, wo_recv,
):
    r, c = lax.axis_index("row"), lax.axis_index("col")
    z, k = lax.div(c, 2), lax.rem(c, 2)
    sigma = 1 - 2 * k
    partner = (r, 2 * z + 1 - k)

    def at_row(d):
        return (lax.rem(r + d, NR), c)

    def at_z(d):
        return (r, 2 * lax.rem(z + d + 2 * NZ, NZ) + k)

    def chip(d):
        return lax.rem(z + sigma * d + NZ, NZ)

    ahead = (r, 2 * chip(1) + k)

    barrier = pltpu.get_barrier_semaphore()

    def greet(d, carry):
        pl.semaphore_signal(barrier, inc=1, device_id=at_row(d), device_id_type=MESH)
        pl.semaphore_signal(barrier, inc=1, device_id=at_z(d), device_id_type=MESH)
        return carry

    lax.fori_loop(1, NR, greet, 0)
    pl.semaphore_signal(barrier, inc=1, device_id=partner, device_id_type=MESH)
    slot_tables(rows, cols, count, table)
    to_idx = pltpu.make_async_copy(table, idx, idx_sem)
    to_idx.start()
    panel[r] = feat[...]
    acc[SLOTS] = jnp.zeros((2, T, H), F32)
    pl.semaphore_wait(barrier, 2 * (NR - 1) + 1)

    def gather(d):
        return remote(feat, panel.at[r], g_send.at[d], g_recv.at[d], at_row(d))

    def gather_from(d):
        return remote(
            feat, panel.at[lax.rem(r - d + NR, NR)], g_send.at[d], g_recv.at[d], at_row(d)
        )

    lax.fori_loop(1, NR, lambda d, u: (gather(d).start(), u)[1], 0)
    to_idx.wait()
    lax.fori_loop(1, NR, lambda d, u: (gather_from(d).wait_recv(), u)[1], 0)

    def add_forward(i, carry):
        for j in range(4):
            s = 4 * i + j
            product = jnp.dot(vals[s], panel[idx[5, s]], preferred_element_type=F32)
            before = idx[0, s]
            for h in range(2):
                acc[s, h] = acc[before, h] + product[:, h * H : (h + 1) * H]
        return carry

    lax.fori_loop(0, SLOTS // 4, add_forward, 0)

    def pair(d):
        return remote(pair_out.at[d], pair_in.at[d], p_send.at[d], p_recv.at[d], partner)

    def hand_over(i, carry):
        d = 8 - i
        for ct in range(2):
            last = idx[1, 2 * chip(-d) + ct]
            for h in range(2):
                pair_out[d, ct, h] = acc[last, h].astype(BF)
        pair(d).start()
        return carry

    lax.fori_loop(0, 8, hand_over, 0)
    theirs = idx[1, 2 * z + 1 - k]
    for h in range(2):
        own_out[h] = acc[theirs, h].astype(BF)
    own_copy = remote(own_out, own_in, o_send, o_recv, partner)
    own_copy.start()

    def link(s, ct, h):
        return remote(
            chain.at[s - 1, ct, h], chain.at[s, ct, h], c_send.at[s, ct, h], c_recv.at[s, ct, h], ahead
        )

    pair(8).wait_recv()
    starts = [
        remote(first.at[ct], chain.at[1, ct, k], f_send.at[ct], c_recv.at[1, ct, k], ahead)
        for ct in range(2)
    ]
    for ct in range(2):
        last = idx[1, 2 * chip(8) + ct]
        first[ct] = (acc[last, k] + pair_in[8, ct, k].astype(F32)).astype(BF)
        starts[ct].start()

    pair(7).wait_recv()
    for ct in range(2):
        last = idx[1, 2 * chip(7) + ct]
        chain[1, ct, 1 - k] = (acc[last, 1 - k] + pair_in[7, ct, 1 - k].astype(F32)).astype(BF)
        link(2, ct, 1 - k).start()
    for ct in range(2):
        last = idx[1, 2 * chip(7) + ct]
        starts[ct].wait_recv()
        chain[1, ct, k] = (
            acc[last, k] + pair_in[7, ct, k].astype(F32) + chain[1, ct, k].astype(F32)
        ).astype(BF)
        link(2, ct, k).start()

    def pass_on(s, carry):
        d = 9 - s
        pair(d).wait_recv()
        for h in range(2):
            for ct in range(2):
                last = idx[1, 2 * chip(d) + ct]
                link(s - 1, ct, h).wait_recv()
                chain[s - 1, ct, h] = (
                    acc[last, h] + pair_in[d, ct, h].astype(F32) + chain[s - 1, ct, h].astype(F32)
                ).astype(BF)
                link(s, ct, h).start()
        return carry

    lax.fori_loop(3, 9, pass_on, 0)

    def side(h):
        return remote(chain.at[8, 1 - k, h], side_in.at[h], f_send.at[2 + h], f_recv.at[h], partner)

    for h in range(2):
        link(8, 1 - k, h).wait_recv()
        side(h).start()
    own_copy.wait_recv()
    mine = idx[1, 2 * z + k]
    halves = []
    for h in range(2):
        link(8, k, h).wait_recv()
        halves.append(acc[mine, h] + own_in[h].astype(F32) + chain[8, k, h].astype(F32))
    for h in range(2):
        side(h).wait_recv()
        halves[h] = (halves[h] + side_in[h].astype(F32)).astype(BF)
    aggregated = jnp.concatenate(halves, axis=1)

    preact = jnp.dot(aggregated, weight[...], preferred_element_type=F32)
    logistic = jax.nn.sigmoid(preact)
    pre_grad = (cot[...].astype(F32) * logistic * (1.0 + preact * (1.0 - logistic))).astype(BF)
    aggregate_grad = lax.dot_general(
        pre_grad, weight[...], (((1,), (1,)), ((), ())), preferred_element_type=F32
    ).astype(BF)

    for h in range(2):
        grads[z, k, h] = aggregate_grad[:, h * H : (h + 1) * H]

    def onward(s, ct, h):
        tile = grads.at[chip(1 - s), ct, h]
        return remote(tile, tile, a_send.at[s, ct, h], a_recv.at[s, ct, h], ahead)

    def arrival(s, ct, h):
        tile = grads.at[chip(-s), ct, h]
        return remote(tile, tile, a_send.at[s, ct, h], a_recv.at[s, ct, h], ahead)

    twin = remote(grads.at[z, k], grads.at[z, k], q_send.at[0, 0], q_recv.at[0, 0], partner)
    twin_in = remote(grads.at[z, 1 - k], grads.at[z, 1 - k], q_send.at[0, 0], q_recv.at[0, 0], partner)
    twin.start()
    for h in range(2):
        onward(1, k, h).start()
    out[...] = (preact * logistic).astype(BF)
    local_grad = lax.dot_general(
        aggregated, pre_grad, (((0,), (0,)), ((), ())), preferred_element_type=F32
    )
    w_loc[...] = local_grad
    for q in range(2):
        for p in range(NR):
            at = q * 128 + (p // 2) * 16
            w_sum[q, p] = w_loc[at : at + 16, (p % 2) * H : (p % 2 + 1) * H].astype(BF)
    twin_in.wait_recv()
    for h in range(2):
        onward(1, 1 - k, h).start()
    w_swap = remote(w_sum.at[1 - k], w_pair, wp_send, wp_recv, partner)
    w_swap.start()

    def both(s):
        there, here = grads.at[chip(-s)], grads.at[chip(s)]
        return (
            remote(there, there, q_send.at[s, 0], q_recv.at[s, 0], partner),
            remote(here, here, q_send.at[s, 0], q_recv.at[s, 0], partner),
        )

    def far(ct):
        there, here = grads.at[chip(8), ct, k], grads.at[chip(8), ct, 1 - k]
        return (
            remote(there, there, q_send.at[8, ct], q_recv.at[8, ct], partner),
            remote(here, here, q_send.at[8, ct], q_recv.at[8, ct], partner),
        )

    def advance(s):
        for ct in (k, 1 - k):
            for h in range(2):
                arrival(s, ct, h).wait_recv()
                if s < 7:
                    onward(s + 1, ct, h).start()
            if s == 7:
                onward(8, ct, k).start()
        both(s)[0].start()

    def w_spread(d):
        return remote(
            w_sum.at[k, lax.rem(r + d, NR)], w_x.at[d], wx_send.at[d], wx_recv.at[d], at_row(d)
        )

    def w_along(d):
        return remote(w_z.at[z], w_z.at[z], wz_send.at[d], wz_recv.at[d], at_z(d))

    def w_along_in(d):
        there = w_z.at[lax.rem(z - d + NZ, NZ)]
        return remote(there, there, wz_send.at[d], wz_recv.at[d], at_z(d))

    def w_share(d):
        return remote(w_all.at[r], w_all.at[r], wa_send.at[d], wa_recv.at[d], at_row(d))

    def w_share_in(d):
        there = w_all.at[lax.rem(r - d + NR, NR)]
        return remote(there, there, wa_send.at[d], wa_recv.at[d], at_row(d))

    def each(make, act):
        lax.fori_loop(1, NR, lambda d, u: (act(make(d)), u)[1], 0)

    def start(copy):
        copy.start()

    def landed(copy):
        copy.wait_recv()

    def sent(copy):
        copy.wait_send()

    advance(1)
    w_swap.wait()
    w_sum[k] = (w_sum[k].astype(F32) + w_pair[...].astype(F32)).astype(BF)
    each(w_spread, start)
    advance(2)
    advance(3)
    each(w_spread, landed)
    part = lax.fori_loop(
        1, NR, lambda d, total: total + w_x[d].astype(F32), w_sum[k, r].astype(F32)
    )
    w_z[z] = part.astype(BF)
    each(w_along, start)
    advance(4)
    advance(5)
    advance(6)
    each(w_along_in, landed)
    whole = lax.fori_loop(
        1, NZ, lambda i, total: total + w_z[i].astype(F32), w_z[0].astype(F32)
    )
    w_all[r] = whole * (1.0 / math.sqrt(NR * 2 * NZ * T))
    each(w_share, start)
    advance(7)
    for ct in range(2):
        arrival(8, ct, k).wait_recv()
        far(ct)[0].start()
    for s in range(1, 8):
        both(s)[1].wait_recv()
    for ct in range(2):
        far(ct)[1].wait_recv()

    def add_backward(i, carry):
        for j in range(4):
            s = 4 * i + j
            row = idx[4, s]
            top, ct = lax.div(row, 2), lax.rem(row, 2)
            tile = jnp.concatenate([grads[top, ct, 0], grads[top, ct, 1]], axis=1)
            product = lax.dot_general(
                vals[s], tile, (((0,), (0,)), ((), ())), preferred_element_type=F32
            )
            before = idx[2, s]
            for h in range(2):
                acc[s, h] = acc[before, h] + product[:, h * H : (h + 1) * H]
        return carry

    lax.fori_loop(0, SLOTS // 4, add_backward, 0)

    def back(d):
        return remote(back_out.at[d], back_in.at[d], b_send.at[d], b_recv.at[d], at_row(d))

    def give_back(d, carry):
        last = idx[3, lax.rem(r + d, NR)]
        for h in range(2):
            back_out[d, :, h * H : (h + 1) * H] = acc[last, h].astype(BF)
        back(d).start()
        return carry

    lax.fori_loop(1, NR, give_back, 0)

    each(w_share_in, landed)
    w_far = remote(w_all, w_other, wo_send, wo_recv, partner)
    w_far.start()
    for p in range(NR):
        at = pl.multiple_of(k * 128 + (p // 2) * 16, 16)
        wgrad[pl.ds(at, 16), (p % 2) * H : (p % 2 + 1) * H] = w_all[p]
    w_far.wait_recv()
    for p in range(NR):
        at = pl.multiple_of((1 - k) * 128 + (p // 2) * 16, 16)
        wgrad[pl.ds(at, 16), (p % 2) * H : (p % 2 + 1) * H] = w_other[p]

    each(gather, sent)
    for d in range(1, 9):
        pair(d).wait_send()
    own_copy.wait_send()
    for ct in range(2):
        starts[ct].wait_send()
        side(ct).wait_send()
        far(ct)[0].wait_send()
        onward(8, ct, k).wait_send()
    for s in range(1, 8):
        both(s)[0].wait_send()
        for ct in range(2):
            for h in range(2):
                link(s + 1, ct, h).wait_send()
                onward(s, ct, h).wait_send()
    twin.wait_send()
    each(w_spread, sent)
    each(w_along, sent)
    each(w_share, sent)
    w_far.wait_send()

    each(back, landed)
    last = idx[3, r]
    for h in range(2):
        cut = slice(h * H, (h + 1) * H)
        total = lax.fori_loop(
            1, NR, lambda d, total: total + back_in[d, :, cut].astype(F32), acc[last, h]
        )
        fgrad[:, cut] = total.astype(BF)
    each(back, sent)


def on_device(features, weight, tile_values, tile_rows, tile_cols, tile_count, cotangent):
    width = features.shape[1]
    dma = pltpu.SemaphoreType.DMA
    vmem = pltpu.VMEM
    return pl.pallas_call(
        kernel,
        out_shape=(
            jax.ShapeDtypeStruct((T, width), BF),
            jax.ShapeDtypeStruct((T, width), BF),
            jax.ShapeDtypeStruct((width, width), F32),
        ),
        in_specs=[pl.BlockSpec(memory_space=pltpu.VMEM)] * 7,
        out_specs=(pl.BlockSpec(memory_space=pltpu.VMEM),) * 3,
        scratch_shapes=[
            vmem((8, 128), jnp.int32),
            pltpu.SMEM((8, 128), jnp.int32),
            vmem((COL_T, T, width), BF),
            vmem((SLOTS + 1, 2, T, H), F32),
            vmem((9, 2, 2, T, H), BF),
            vmem((9, 2, 2, T, H), BF),
            vmem((2, T, H), BF),
            vmem((2, T, H), BF),
            vmem((2, T, H), BF),
            vmem((9, 2, 2, T, H), BF),
            vmem((2, T, H), BF),
            vmem((NZ, 2, 2, T, H), BF),
            vmem((NR, T, width), BF),
            vmem((NR, T, width), BF),
            vmem((width, width), F32),
            vmem((NR, 16, 128), BF),
            vmem((2, NR, 16, 128), BF),
            vmem((NR, 16, 128), BF),
            vmem((NZ, 16, 128), BF),
            vmem((NR, 16, 128), F32),
            vmem((NR, 16, 128), F32),
            dma,
            dma((NR,)), dma((NR,)),
            dma((9,)), dma((9,)),
            dma, dma,
            dma((9, 2, 2)), dma((9, 2, 2)),
            dma((4,)), dma((2,)),
            dma((9, 2, 2)), dma((9, 2, 2)),
            dma((9, 2)), dma((9, 2)),
            dma((NR,)), dma((NR,)),
            dma, dma,
            dma((NR,)), dma((NR,)),
            dma((NZ,)), dma((NZ,)),
            dma((NR,)), dma((NR,)),
            dma, dma,
        ],
        compiler_params=pltpu.CompilerParams(
            collective_id=0, has_side_effects=True, vmem_limit_bytes=48 * 2**20
        ),
    )(
        features,
        weight,
        tile_values.reshape(SLOTS, T, T),
        tile_rows.reshape(1, SLOTS),
        tile_cols.reshape(1, SLOTS),
        tile_count.reshape(1, 1),
        cotangent,
    )


def solution(mesh):
    return jax.shard_map(
        on_device,
        mesh=mesh,
        in_specs=(
            P(("col", "row"), None),
            P(),
            P("row", "col", None, None, None),
            P("row", "col", None),
            P("row", "col", None),
            P("row", "col"),
            P(("row", "col"), None),
        ),
        out_specs=(P(("row", "col"), None), P(("col", "row"), None), P()),
        check_vma=False,
    )
```

```python
import functools
import math

import jax
import jax.numpy as jnp
from jax import lax
from jax.experimental import pallas as pl
from jax.experimental.pallas import tpu as pltpu
from jax.sharding import PartitionSpec as P

MESH = pl.DeviceIdType.MESH
BF = jnp.bfloat16
F32 = jnp.float32
NX, NY, NZ, NR = 4, 4, 16, 16
SLOTS, ROW_T, COL_T, T = 32, 32, 16, 128
H = 128


def remote(src, dst, send, recv, device):
    return pltpu.make_async_remote_copy(
        src_ref=src, dst_ref=dst, send_sem=send, recv_sem=recv, device_id=device, device_id_type=MESH
    )


def slot_tables(rows, cols, count, table):
    sub = lax.broadcasted_iota(jnp.int32, (SLOTS, SLOTS), 0)
    lane = lax.broadcasted_iota(jnp.int32, (SLOTS, SLOTS), 1)
    used = sub < count

    def latest(mask):
        found = jnp.max(jnp.where(mask, sub, -1), axis=0, keepdims=True)
        return jnp.where(found < 0, SLOTS, found)

    for base, ref in ((0, rows), (2, cols)):
        along = jnp.broadcast_to(ref[...], (SLOTS, SLOTS))
        down = jnp.sum(jnp.where(sub == lane, along, 0), axis=1, keepdims=True)
        table[base : base + 1, :SLOTS] = latest((down == along) & (sub < lane) & used)
        table[base + 1 : base + 2, :SLOTS] = latest((down == lane) & used)
        table[4 + base // 2 : 5 + base // 2, :SLOTS] = ref[...]


def kernel(
    feat, weight_hbm, vals_hbm, rows_hbm, cols_hbm, count, cot_hbm, out, fgrad, wgrad,
    weight, vals, rows, cols, cot, table, idx, panel_a, panel_b, acc, pair_out, pair_in, own_out, own_in, first, leaf_out,
    chain_in, leaf_in, side_out, side_in, grads_a, grads_b, back_out, back_in,
    w_loc, w_pair, w_sum, w_x, w_z, w_all, w_other,
    in_sem, idx_sem, g_send, g_recv, p_send, p_recv, o_send, o_recv, c_send, c_recv, l_send, l_recv, f_send, f_recv,
    a_send, a_recv, al_send, al_recv, q_send, q_recv, ql_send, ql_recv, t_send, t_recv, b_send, b_recv,
    wp_send, wp_recv, wx_send, wx_recv, wz_send, wz_recv, wa_send, wa_recv, wo_send, wo_recv,
):
    panel, grads = (panel_a, panel_b), (grads_a, grads_b)
    r, c = lax.axis_index("row"), lax.axis_index("col")
    z, k = lax.div(c, 2), lax.rem(c, 2)
    other = 1 - k
    sigma = 1 - 2 * k
    partner = (r, 2 * z + other)

    def at_row(d):
        return (lax.rem(r + d, NR), c)

    def at_z(d):
        return (r, 2 * lax.rem(z + d, NZ) + k)

    chips = {d: lax.rem(z + sigma * d + NZ, NZ) for d in range(-8, 9)}
    one, two = (r, 2 * chips[1] + k), (r, 2 * chips[2] + k)
    sent = []

    def start(copy):
        copy.start()
        sent.append(copy)

    def each(make, act):
        lax.fori_loop(1, NR, lambda d, u: (act(make(d)), u)[1], 0)

    def begin(copy):
        copy.start()

    def landed(copy):
        copy.wait_recv()

    def gone(copy):
        copy.wait_send()

    loads = [
        pltpu.make_async_copy(rows_hbm, rows, in_sem.at[0]),
        pltpu.make_async_copy(cols_hbm, cols, in_sem.at[1]),
        pltpu.make_async_copy(feat.at[:, 0:H], panel[0].at[r], in_sem.at[2]),
        pltpu.make_async_copy(feat.at[:, H : 2 * H], panel[1].at[r], in_sem.at[3]),
        pltpu.make_async_copy(vals_hbm, vals, in_sem.at[4]),
        pltpu.make_async_copy(weight_hbm, weight, in_sem.at[5]),
        pltpu.make_async_copy(cot_hbm, cot, in_sem.at[6]),
    ]
    for load in loads:
        load.start()
    barrier = pltpu.get_barrier_semaphore()

    def greet(d, carry):
        pl.semaphore_signal(barrier, inc=1, device_id=at_z(d), device_id_type=MESH)
        pl.semaphore_signal(barrier, inc=1, device_id=at_row(d), device_id_type=MESH)
        return carry

    lax.fori_loop(1, NR, greet, 0)
    pl.semaphore_signal(barrier, inc=1, device_id=partner, device_id_type=MESH)
    for h in range(2):
        acc[h, SLOTS] = jnp.zeros((T, H), F32)
    loads[0].wait()
    loads[1].wait()
    slot_tables(rows, cols, count[0, 0], table)
    to_idx = pltpu.make_async_copy(table, idx, idx_sem)
    to_idx.start()
    for load in loads[2:]:
        load.wait()
    to_idx.wait()
    pl.semaphore_wait(barrier, 2 * (NR - 1) + 1)

    def gather(h):
        mine = panel[h].at[r]
        return lambda d: remote(mine, mine, g_send.at[h, d], g_recv.at[h, d], at_row(d))

    def gathered(h):
        def make(d):
            theirs = panel[h].at[lax.rem(r - d + NR, NR)]
            return remote(theirs, theirs, g_send.at[h, d], g_recv.at[h, d], at_row(d))

        return make

    for h in range(2):
        each(gather(h), begin)

    def forward(h):
        each(gathered(h), landed)

        def step(i, carry):
            for j in range(8):
                s = 8 * i + j
                acc[h, s] = acc[h, idx[0, s]] + jnp.dot(
                    vals[s], panel[h][idx[5, s]], preferred_element_type=F32
                )
            return carry

        lax.fori_loop(0, SLOTS // 8, step, 0)

    def pair(h, g):
        return remote(pair_out.at[h, g], pair_in.at[h, g], p_send.at[h, g], p_recv.at[h, g], partner)

    def own_copy(h):
        return remote(own_out.at[h], own_in.at[h], o_send.at[h], o_recv.at[h], partner)

    def hand_over(h):
        for g in range(4):
            for j in range(2):
                for ct in range(2):
                    last = idx[1, 2 * chips[2 * g + j - 8] + ct]
                    pair_out[h, g, j, ct] = acc[h, last].astype(BF)
            start(pair(h, g))
        own_out[h] = acc[h, idx[1, 2 * z + other]].astype(BF)
        start(own_copy(h))

    def both(h, d, ct):
        last = idx[1, 2 * chips[d] + ct]
        return acc[h, last] + pair_in[h, (8 - d) // 2, (8 - d) % 2, ct].astype(F32)

    def link(h, s, ct):
        source = first.at[h] if s == 1 else chain_in.at[h, s - 2, ct]
        return remote(
            source, chain_in.at[h, s - 1, ct], c_send.at[h, s - 1, ct], c_recv.at[h, s - 1, ct], two
        )

    def leaf(h, i):
        return remote(leaf_out.at[h, i], leaf_in.at[h, i], l_send.at[h, i], l_recv.at[h, i], one)

    def send_leaf(h, i):
        for ct in range(2):
            leaf_out[h, i, ct] = both(h, 7 - 2 * i, ct).astype(BF)
        start(leaf(h, i))

    def sums_begin(h):
        pair(h, 0).wait_recv()
        first[h] = both(h, 8, k).astype(BF)
        start(link(h, 1, k))
        send_leaf(h, 0)

    def sums_step(h, s):
        pair(h, s - 1).wait_recv()
        leaf(h, s - 2).wait_recv()
        for ct in (other, k):
            total = both(h, 10 - 2 * s, ct) + leaf_in[h, s - 2, ct].astype(F32)
            if s > 2 or ct is k:
                link(h, s - 1, ct).wait_recv()
                total = total + chain_in[h, s - 2, ct].astype(F32)
            chain_in[h, s - 2, ct] = total.astype(BF)
            start(link(h, s, ct))
        send_leaf(h, s - 1)

    def side(h):
        return remote(side_out.at[h], side_in.at[h], f_send.at[h], f_recv.at[h], partner)

    def sums_end(h):
        leaf(h, 3).wait_recv()
        link(h, 4, other).wait_recv()
        side_out[h] = (chain_in[h, 3, other].astype(F32) + leaf_in[h, 3, other].astype(F32)).astype(BF)
        start(side(h))
        own_copy(h).wait_recv()
        link(h, 4, k).wait_recv()
        return (
            acc[h, idx[1, 2 * z + k]]
            + own_in[h].astype(F32)
            + chain_in[h, 3, k].astype(F32)
            + leaf_in[h, 3, k].astype(F32)
        )

    forward(0)
    hand_over(0)
    sums_begin(0)
    forward(1)
    hand_over(1)
    sums_begin(1)
    for s in range(2, 5):
        sums_step(0, s)
        sums_step(1, s)
    halves = [sums_end(0), sums_end(1)]
    for h in range(2):
        side(h).wait_recv()
        halves[h] = (halves[h] + side_in[h].astype(F32)).astype(BF)
    aggregated = jnp.concatenate(halves, axis=1)

    preact = jnp.dot(aggregated, weight[...], preferred_element_type=F32)
    logistic = jax.nn.sigmoid(preact)
    pre_grad = (cot[...].astype(F32) * logistic * (1.0 + preact * (1.0 - logistic))).astype(BF)

    def twin(h, ct):
        tile = grads[h].at[z, ct]
        return remote(tile, tile, t_send.at[h], t_recv.at[h], partner)

    def chain(h, s, ct, at):
        tile = grads[h].at[at, ct]
        return remote(tile, tile, a_send.at[h, s - 1, ct], a_recv.at[h, s - 1, ct], two)

    def twig(h, s, at):
        tiles = grads[h].at[at]
        return remote(tiles, tiles, al_send.at[h, s - 1], al_recv.at[h, s - 1], one)

    def share(h, s, at):
        tiles = grads[h].at[at]
        return remote(tiles, tiles, q_send.at[h, s - 1], q_recv.at[h, s - 1], partner)

    def share_far(h, ct):
        tile = grads[h].at[chips[8], ct]
        return remote(tile, tile, q_send.at[h, 3], q_recv.at[h, 3], partner)

    def share_twig(h, s, at):
        tiles = grads[h].at[at]
        return remote(tiles, tiles, ql_send.at[h, s - 1], ql_recv.at[h, s - 1], partner)

    for h in range(2):
        grads[h][z, k] = lax.dot_general(
            pre_grad, weight[h * H : (h + 1) * H, :], (((1,), (1,)), ((), ())), preferred_element_type=F32
        ).astype(BF)
        start(twin(h, k))
        start(chain(h, 1, k, z))
    for h in range(2):
        twin(h, other).wait_recv()
        start(chain(h, 1, other, z))
        start(twig(h, 1, z))
    out[...] = (preact * logistic).astype(BF)
    w_loc[...] = lax.dot_general(
        aggregated, pre_grad, (((0,), (0,)), ((), ())), preferred_element_type=F32
    )
    for q in range(2):
        for p in range(NR):
            at = q * 128 + (p // 2) * 16
            w_sum[q, p] = w_loc[at : at + 16, (p % 2) * H : (p % 2 + 1) * H].astype(BF)
    w_swap = remote(w_sum.at[other], w_pair, wp_send, wp_recv, partner)
    w_swap.start()

    def advance(h, s):
        at = chips[-2 * s]
        if s < 4:
            for ct in (k, other):
                chain(h, s, ct, at).wait_recv()
                if s < 3 or ct is k:
                    start(chain(h, s + 1, ct, at))
            start(twig(h, s + 1, at))
            start(share(h, s, at))
        else:
            chain(h, 4, k, at).wait_recv()
            start(share_far(h, k))
        twig(h, s, chips[1 - 2 * s]).wait_recv()
        start(share_twig(h, s, chips[1 - 2 * s]))

    def shared(h):
        for s in range(1, 4):
            share(h, s, chips[2 * s]).wait_recv()
            share_twig(h, s, chips[2 * s - 1]).wait_recv()
        share_far(h, other).wait_recv()
        share_twig(h, 4, chips[7]).wait_recv()

    def w_spread(d):
        return remote(
            w_sum.at[k, lax.rem(r + d, NR)], w_x.at[d], wx_send.at[d], wx_recv.at[d], at_row(d)
        )

    def w_along(d):
        return remote(w_z.at[z], w_z.at[z], wz_send.at[d], wz_recv.at[d], at_z(d))

    def w_along_in(d):
        there = w_z.at[lax.rem(z - d + NZ, NZ)]
        return remote(there, there, wz_send.at[d], wz_recv.at[d], at_z(d))

    def w_share(d):
        return remote(w_all.at[r], w_all.at[r], wa_send.at[d], wa_recv.at[d], at_row(d))

    def w_share_in(d):
        there = w_all.at[lax.rem(r - d + NR, NR)]
        return remote(there, there, wa_send.at[d], wa_recv.at[d], at_row(d))

    def backward(h):
        def step(i, carry):
            for j in range(8):
                s = 8 * i + j
                row = idx[4, s]
                acc[h, s] = acc[h, idx[2, s]] + lax.dot_general(
                    vals[s],
                    grads[h][lax.div(row, 2), lax.rem(row, 2)],
                    (((0,), (0,)), ((), ())),
                    preferred_element_type=F32,
                )
            return carry

        lax.fori_loop(0, SLOTS // 8, step, 0)

        def give_back(d, carry):
            back_out[h, d] = acc[h, idx[3, lax.rem(r + d, NR)]].astype(BF)
            back(h)(d).start()
            return carry

        lax.fori_loop(1, NR, give_back, 0)

    def back(h):
        return lambda d: remote(
            back_out.at[h, d], back_in.at[h, d], b_send.at[h, d], b_recv.at[h, d], at_row(d)
        )

    def back_end(h):
        each(back(h), landed)
        total = lax.fori_loop(
            1, NR, lambda d, total: total + back_in[h, d].astype(F32), acc[h, idx[3, r]]
        )
        fgrad[:, h * H : (h + 1) * H] = total.astype(BF)

    advance(0, 1)
    w_swap.wait()
    w_sum[k] = (w_sum[k].astype(F32) + w_pair[...].astype(F32)).astype(BF)
    advance(1, 1)
    each(w_spread, begin)
    advance(0, 2)
    advance(1, 2)
    each(w_spread, landed)
    part = lax.fori_loop(
        1, NR, lambda d, total: total + w_x[d].astype(F32), w_sum[k, r].astype(F32)
    )
    w_z[z] = part.astype(BF)
    each(w_along, begin)
    advance(0, 3)
    advance(1, 3)
    advance(0, 4)
    shared(0)
    backward(0)
    advance(1, 4)
    each(w_along_in, landed)
    whole = lax.fori_loop(
        1, NZ, lambda i, total: total + w_z[i].astype(F32), w_z[0].astype(F32)
    )
    w_all[r] = whole * (1.0 / math.sqrt(NR * 2 * NZ * T))
    each(w_share, begin)
    shared(1)
    backward(1)

    each(w_share_in, landed)
    w_far = remote(w_all, w_other, wo_send, wo_recv, partner)
    w_far.start()
    for p in range(NR):
        at = pl.multiple_of(k * 128 + (p // 2) * 16, 16)
        wgrad[pl.ds(at, 16), (p % 2) * H : (p % 2 + 1) * H] = w_all[p]
    back_end(0)
    w_far.wait()
    for p in range(NR):
        at = pl.multiple_of(other * 128 + (p // 2) * 16, 16)
        wgrad[pl.ds(at, 16), (p % 2) * H : (p % 2 + 1) * H] = w_other[p]

    for copy in sent:
        copy.wait_send()
    for make in (gather(0), gather(1), w_spread, w_along, w_share):
        each(make, gone)
    back_end(1)
    for h in range(2):
        each(back(h), gone)


def in_hbm(array):
    return pltpu.with_memory_space_constraint(array, pltpu.HBM)


def on_device(features, weight, tile_values, tile_rows, tile_cols, tile_count, cotangent):
    width = features.shape[1]
    dma = pltpu.SemaphoreType.DMA
    vmem = pltpu.VMEM
    hbm = pl.BlockSpec(memory_space=pltpu.HBM)
    return pl.pallas_call(
        kernel,
        out_shape=(
            jax.ShapeDtypeStruct((T, width), BF),
            jax.ShapeDtypeStruct((T, width), BF),
            jax.ShapeDtypeStruct((width, width), F32),
        ),
        in_specs=[hbm] * 5 + [pl.BlockSpec(memory_space=pltpu.SMEM), hbm],
        out_specs=(pl.BlockSpec(memory_space=pltpu.VMEM),) * 3,
        scratch_shapes=[
            vmem((width, width), BF),
            vmem((SLOTS, T, T), BF),
            vmem((1, SLOTS), jnp.int32),
            vmem((1, SLOTS), jnp.int32),
            vmem((T, width), BF),
            vmem((8, 128), jnp.int32),
            pltpu.SMEM((8, 128), jnp.int32),
            vmem((COL_T, T, H), BF),
            vmem((COL_T, T, H), BF),
            vmem((2, SLOTS + 1, T, H), F32),
            vmem((2, 4, 2, 2, T, H), BF),
            vmem((2, 4, 2, 2, T, H), BF),
            vmem((2, T, H), BF),
            vmem((2, T, H), BF),
            vmem((2, T, H), BF),
            vmem((2, 4, 2, T, H), BF),
            vmem((2, 4, 2, T, H), BF),
            vmem((2, 4, 2, T, H), BF),
            vmem((2, T, H), BF),
            vmem((2, T, H), BF),
            vmem((NZ, 2, T, H), BF),
            vmem((NZ, 2, T, H), BF),
            vmem((2, NR, T, H), BF),
            vmem((2, NR, T, H), BF),
            vmem((width, width), F32),
            vmem((NR, 16, 128), BF),
            vmem((2, NR, 16, 128), BF),
            vmem((NR, 16, 128), BF),
            vmem((NZ, 16, 128), BF),
            vmem((NR, 16, 128), F32),
            vmem((NR, 16, 128), F32),
            dma((7,)),
            dma,
            dma((2, NR)), dma((2, NR)),
            dma((2, 4)), dma((2, 4)),
            dma((2,)), dma((2,)),
            dma((2, 4, 2)), dma((2, 4, 2)),
            dma((2, 4)), dma((2, 4)),
            dma((2,)), dma((2,)),
            dma((2, 4, 2)), dma((2, 4, 2)),
            dma((2, 4)), dma((2, 4)),
            dma((2, 4)), dma((2, 4)),
            dma((2, 4)), dma((2, 4)),
            dma((2,)), dma((2,)),
            dma((2, NR)), dma((2, NR)),
            dma, dma,
            dma((NR,)), dma((NR,)),
            dma((NZ,)), dma((NZ,)),
            dma((NR,)), dma((NR,)),
            dma, dma,
        ],
        compiler_params=pltpu.CompilerParams(
            collective_id=0, has_side_effects=True, vmem_limit_bytes=48 * 2**20
        ),
    )(
        in_hbm(features),
        in_hbm(weight),
        in_hbm(tile_values.reshape(SLOTS, T, T)),
        in_hbm(tile_rows.reshape(1, SLOTS)),
        in_hbm(tile_cols.reshape(1, SLOTS)),
        tile_count,
        in_hbm(cotangent),
    )


def solution(mesh):
    return jax.shard_map(
        on_device,
        mesh=mesh,
        in_specs=(
            P(("col", "row"), None),
            P(),
            P("row", "col", None, None, None),
            P("row", "col", None),
            P("row", "col", None),
            P("row", "col"),
            P(("row", "col"), None),
        ),
        out_specs=(P(("row", "col"), None), P(("col", "row"), None), P()),
        check_vma=False,
    )
```

```python
import functools
import math

import jax
import jax.numpy as jnp
from jax import lax
from jax.experimental import pallas as pl
from jax.experimental.pallas import tpu as pltpu
from jax.sharding import PartitionSpec as P

MESH = pl.DeviceIdType.MESH
BF = jnp.bfloat16
F32 = jnp.float32
NX, NY, NZ, NR = 4, 4, 16, 16
SLOTS, ROW_T, COL_T, T = 32, 32, 16, 128
H = 128


def remote(src, dst, send, recv, device):
    return pltpu.make_async_remote_copy(
        src_ref=src, dst_ref=dst, send_sem=send, recv_sem=recv, device_id=device, device_id_type=MESH
    )


def slot_tables(rows, cols, count, table):
    sub = lax.broadcasted_iota(jnp.int32, (SLOTS, SLOTS), 0)
    lane = lax.broadcasted_iota(jnp.int32, (SLOTS, SLOTS), 1)
    used = sub < count

    def latest(mask):
        found = jnp.max(jnp.where(mask, sub, -1), axis=0, keepdims=True)
        return jnp.where(found < 0, SLOTS, found)

    for base, ref in ((0, rows), (2, cols)):
        along = jnp.broadcast_to(ref[...], (SLOTS, SLOTS))
        down = jnp.sum(jnp.where(sub == lane, along, 0), axis=1, keepdims=True)
        table[base : base + 1, :SLOTS] = latest((down == along) & (sub < lane) & used)
        table[base + 1 : base + 2, :SLOTS] = latest((down == lane) & used)
    table[4:5, :SLOTS] = rows[...]
    table[5:6, :SLOTS] = lax.rem(cols[...], NY) * NX + lax.div(cols[...], NY)
    table[6:7, :SLOTS] = cols[...]


def kernel(
    feat, weight_hbm, vals_hbm, rows_hbm, cols_hbm, count, cot_hbm, out, fgrad, wgrad,
    weight, vals, rows, cols, cot, table, idx, panel_a, panel_b, acc, pair_out, pair_in, own_out, own_in, first, leaf_out,
    chain_in, leaf_in, side_out, side_in, grads_a, grads_b, back_out, back_in, mid_out, mid_in,
    w_loc, w_pair, w_sum, w_x, w_z, w_all, w_other,
    in_sem, idx_sem, g_send, g_recv, gb_send, gb_recv, p_send, p_recv, o_send, o_recv, c_send, c_recv, l_send, l_recv, f_send, f_recv,
    a_send, a_recv, al_send, al_recv, q_send, q_recv, ql_send, ql_recv, t_send, t_recv, b_send, b_recv, bm_send, bm_recv,
    wp_send, wp_recv, wx_send, wx_recv, wz_send, wz_recv, wa_send, wa_recv, wo_send, wo_recv,
):
    panel, grads = (panel_a, panel_b), (grads_a, grads_b)
    r, c = lax.axis_index("row"), lax.axis_index("col")
    z, k = lax.div(c, 2), lax.rem(c, 2)
    other = 1 - k
    sigma = 1 - 2 * k
    partner = (r, 2 * z + other)

    x, y = lax.div(r, NY), lax.rem(r, NY)
    line = ((x, y), (y, x))

    def row_of(h, a, b):
        return a * NY + b if h == 0 else b * NY + a

    def along_a(h, e):
        return (row_of(h, lax.rem(line[h][0] + e, NX), line[h][1]), c)

    def along_b(h, e):
        return (row_of(h, line[h][0], lax.rem(line[h][1] + e, NX)), c)

    def at_row(d):
        return (lax.rem(r + d, NR), c)

    def at_z(d):
        return (r, 2 * lax.rem(z + d, NZ) + k)

    chips = {d: lax.rem(z + sigma * d + NZ, NZ) for d in range(-8, 9)}
    one, two = (r, 2 * chips[1] + k), (r, 2 * chips[2] + k)
    sent = []

    def start(copy):
        copy.start()
        sent.append(copy)

    def each(make, act):
        lax.fori_loop(1, NR, lambda d, u: (act(make(d)), u)[1], 0)

    def begin(copy):
        copy.start()

    def landed(copy):
        copy.wait_recv()

    def gone(copy):
        copy.wait_send()

    loads = [
        pltpu.make_async_copy(rows_hbm, rows, in_sem.at[0]),
        pltpu.make_async_copy(cols_hbm, cols, in_sem.at[1]),
        pltpu.make_async_copy(feat.at[:, 0:H], panel[0].at[y * NX + x], in_sem.at[2]),
        pltpu.make_async_copy(feat.at[:, H : 2 * H], panel[1].at[r], in_sem.at[3]),
        pltpu.make_async_copy(vals_hbm, vals, in_sem.at[4]),
        pltpu.make_async_copy(weight_hbm, weight, in_sem.at[5]),
        pltpu.make_async_copy(cot_hbm, cot, in_sem.at[6]),
    ]
    for load in loads:
        load.start()
    barrier = pltpu.get_barrier_semaphore()

    def greet(d, carry):
        pl.semaphore_signal(barrier, inc=1, device_id=at_z(d), device_id_type=MESH)
        pl.semaphore_signal(barrier, inc=1, device_id=at_row(d), device_id_type=MESH)
        return carry

    lax.fori_loop(1, NR, greet, 0)
    pl.semaphore_signal(barrier, inc=1, device_id=partner, device_id_type=MESH)
    for h in range(2):
        acc[h, SLOTS] = jnp.zeros((T, H), F32)
    loads[0].wait()
    loads[1].wait()
    slot_tables(rows, cols, count[0, 0], table)
    to_idx = pltpu.make_async_copy(table, idx, idx_sem)
    to_idx.start()
    for load in loads[2:]:
        load.wait()
    to_idx.wait()
    pl.semaphore_wait(barrier, 2 * (NR - 1) + 1)

    def gather_a(h, e, a):
        tile = panel[h].at[line[h][1] * NX + a]
        return remote(tile, tile, g_send.at[h, e - 1], g_recv.at[h, e - 1], along_a(h, e))

    def gather_b(h, e, b):
        tiles = panel[h].at[pl.ds(b * NX, NX)]
        return remote(tiles, tiles, gb_send.at[h, e - 1], gb_recv.at[h, e - 1], along_b(h, e))

    for h in range(2):
        for e in (2, 1, 3):
            start(gather_a(h, e, line[h][0]))
    for h in range(2):
        for e in (1, 3, 2):
            gather_a(h, e, lax.rem(line[h][0] - e + NX, NX)).wait_recv()
        for e in (2, 1, 3):
            start(gather_b(h, e, line[h][1]))

    def forward(h):
        for e in (1, 3, 2):
            gather_b(h, e, lax.rem(line[h][1] - e + NX, NX)).wait_recv()

        def step(i, carry):
            for j in range(8):
                s = 8 * i + j
                acc[h, s] = acc[h, idx[0, s]] + jnp.dot(
                    vals[s], panel[h][idx[5 + h, s]], preferred_element_type=F32
                )
            return carry

        lax.fori_loop(0, SLOTS // 8, step, 0)

    def pair(h, g):
        return remote(pair_out.at[h, g], pair_in.at[h, g], p_send.at[h, g], p_recv.at[h, g], partner)

    def own_copy(h):
        return remote(own_out.at[h], own_in.at[h], o_send.at[h], o_recv.at[h], partner)

    def hand_over(h):
        for g in range(4):
            for j in range(2):
                for ct in range(2):
                    last = idx[1, 2 * chips[2 * g + j - 8] + ct]
                    pair_out[h, g, j, ct] = acc[h, last].astype(BF)
            start(pair(h, g))
        own_out[h] = acc[h, idx[1, 2 * z + other]].astype(BF)
        start(own_copy(h))

    def both(h, d, ct):
        last = idx[1, 2 * chips[d] + ct]
        return acc[h, last] + pair_in[h, (8 - d) // 2, (8 - d) % 2, ct].astype(F32)

    def link(h, s, ct):
        source = first.at[h] if s == 1 else chain_in.at[h, s - 2, ct]
        return remote(
            source, chain_in.at[h, s - 1, ct], c_send.at[h, s - 1, ct], c_recv.at[h, s - 1, ct], two
        )

    def leaf(h, i):
        return remote(leaf_out.at[h, i], leaf_in.at[h, i], l_send.at[h, i], l_recv.at[h, i], one)

    def send_leaf(h, i):
        for ct in range(2):
            leaf_out[h, i, ct] = both(h, 7 - 2 * i, ct).astype(BF)
        start(leaf(h, i))

    def sums_begin(h):
        pair(h, 0).wait_recv()
        first[h] = both(h, 8, k).astype(BF)
        start(link(h, 1, k))
        send_leaf(h, 0)

    def sums_step(h, s):
        pair(h, s - 1).wait_recv()
        leaf(h, s - 2).wait_recv()
        for ct in (other, k):
            total = both(h, 10 - 2 * s, ct) + leaf_in[h, s - 2, ct].astype(F32)
            if s > 2 or ct is k:
                link(h, s - 1, ct).wait_recv()
                total = total + chain_in[h, s - 2, ct].astype(F32)
            chain_in[h, s - 2, ct] = total.astype(BF)
            start(link(h, s, ct))
        send_leaf(h, s - 1)

    def side(h):
        return remote(side_out.at[h], side_in.at[h], f_send.at[h], f_recv.at[h], partner)

    def sums_end(h):
        leaf(h, 3).wait_recv()
        link(h, 4, other).wait_recv()
        side_out[h] = (chain_in[h, 3, other].astype(F32) + leaf_in[h, 3, other].astype(F32)).astype(BF)
        start(side(h))
        own_copy(h).wait_recv()
        link(h, 4, k).wait_recv()
        return (
            acc[h, idx[1, 2 * z + k]]
            + own_in[h].astype(F32)
            + chain_in[h, 3, k].astype(F32)
            + leaf_in[h, 3, k].astype(F32)
        )

    forward(0)
    hand_over(0)
    sums_begin(0)
    forward(1)
    hand_over(1)
    sums_begin(1)
    for s in range(2, 5):
        sums_step(0, s)
        sums_step(1, s)
    halves = [sums_end(0), sums_end(1)]
    for h in range(2):
        side(h).wait_recv()
        halves[h] = (halves[h] + side_in[h].astype(F32)).astype(BF)
    aggregated = jnp.concatenate(halves, axis=1)

    preact = jnp.dot(aggregated, weight[...], preferred_element_type=F32)
    logistic = jax.nn.sigmoid(preact)
    pre_grad = (cot[...].astype(F32) * logistic * (1.0 + preact * (1.0 - logistic))).astype(BF)

    def twin(h, ct):
        tile = grads[h].at[z, ct]
        return remote(tile, tile, t_send.at[h], t_recv.at[h], partner)

    def chain(h, s, ct, at):
        tile = grads[h].at[at, ct]
        return remote(tile, tile, a_send.at[h, s - 1, ct], a_recv.at[h, s - 1, ct], two)

    def twig(h, s, at):
        tiles = grads[h].at[at]
        return remote(tiles, tiles, al_send.at[h, s - 1], al_recv.at[h, s - 1], one)

    def share(h, s, at):
        tiles = grads[h].at[at]
        return remote(tiles, tiles, q_send.at[h, s - 1], q_recv.at[h, s - 1], partner)

    def share_far(h, ct):
        tile = grads[h].at[chips[8], ct]
        return remote(tile, tile, q_send.at[h, 3], q_recv.at[h, 3], partner)

    def share_twig(h, s, at):
        tiles = grads[h].at[at]
        return remote(tiles, tiles, ql_send.at[h, s - 1], ql_recv.at[h, s - 1], partner)

    for h in range(2):
        grads[h][z, k] = lax.dot_general(
            pre_grad, weight[h * H : (h + 1) * H, :], (((1,), (1,)), ((), ())), preferred_element_type=F32
        ).astype(BF)
        start(twin(h, k))
        start(chain(h, 1, k, z))
    for h in range(2):
        twin(h, other).wait_recv()
        start(chain(h, 1, other, z))
        start(twig(h, 1, z))
    out[...] = (preact * logistic).astype(BF)
    w_loc[...] = lax.dot_general(
        aggregated, pre_grad, (((0,), (0,)), ((), ())), preferred_element_type=F32
    )
    for q in range(2):
        for p in range(NR):
            at = q * 128 + (p // 2) * 16
            w_sum[q, p] = w_loc[at : at + 16, (p % 2) * H : (p % 2 + 1) * H].astype(BF)
    w_swap = remote(w_sum.at[other], w_pair, wp_send, wp_recv, partner)
    w_swap.start()

    def advance(h, s):
        at = chips[-2 * s]
        if s < 4:
            for ct in (k, other):
                chain(h, s, ct, at).wait_recv()
                if s < 3 or ct is k:
                    start(chain(h, s + 1, ct, at))
            start(twig(h, s + 1, at))
            start(share(h, s, at))
        else:
            chain(h, 4, k, at).wait_recv()
            start(share_far(h, k))
        twig(h, s, chips[1 - 2 * s]).wait_recv()
        start(share_twig(h, s, chips[1 - 2 * s]))

    def shared(h):
        for s in range(1, 4):
            share(h, s, chips[2 * s]).wait_recv()
            share_twig(h, s, chips[2 * s - 1]).wait_recv()
        share_far(h, other).wait_recv()
        share_twig(h, 4, chips[7]).wait_recv()

    def w_spread(d):
        return remote(
            w_sum.at[k, lax.rem(r + d, NR)], w_x.at[d], wx_send.at[d], wx_recv.at[d], at_row(d)
        )

    def w_along(d):
        return remote(w_z.at[z], w_z.at[z], wz_send.at[d], wz_recv.at[d], at_z(d))

    def w_along_in(d):
        there = w_z.at[lax.rem(z - d + NZ, NZ)]
        return remote(there, there, wz_send.at[d], wz_recv.at[d], at_z(d))

    def w_share(d):
        return remote(w_all.at[r], w_all.at[r], wa_send.at[d], wa_recv.at[d], at_row(d))

    def w_share_in(d):
        there = w_all.at[lax.rem(r - d + NR, NR)]
        return remote(there, there, wa_send.at[d], wa_recv.at[d], at_row(d))

    def backward(h):
        def step(i, carry):
            for j in range(8):
                s = 8 * i + j
                row = idx[4, s]
                acc[h, s] = acc[h, idx[2, s]] + lax.dot_general(
                    vals[s],
                    grads[h][lax.div(row, 2), lax.rem(row, 2)],
                    (((0,), (0,)), ((), ())),
                    preferred_element_type=F32,
                )
            return carry

        lax.fori_loop(0, SLOTS // 8, step, 0)

        for e in (2, 1, 3):
            for a in range(NX):
                last = idx[3, row_of(h, a, lax.rem(line[h][1] + e, NX))]
                back_out[h, e - 1, a] = acc[h, last].astype(BF)
            start(back(h, e))

    def back(h, e):
        return remote(
            back_out.at[h, e - 1], back_in.at[h, e - 1], b_send.at[h, e - 1], b_recv.at[h, e - 1], along_b(h, e)
        )

    def middle(h, e):
        return remote(
            mid_out.at[h, e - 1], mid_in.at[h, e - 1], bm_send.at[h, e - 1], bm_recv.at[h, e - 1], along_a(h, e)
        )

    def line_sum(h, a):
        total = acc[h, idx[3, row_of(h, a, line[h][1])]]
        for e in range(3):
            total = total + back_in[h, e, a].astype(F32)
        return total

    def back_middle(h):
        for e in (1, 3, 2):
            back(h, e).wait_recv()
        for e in (2, 1, 3):
            mid_out[h, e - 1] = line_sum(h, lax.rem(line[h][0] + e, NX)).astype(BF)
            start(middle(h, e))

    def back_end(h):
        total = line_sum(h, line[h][0])
        for e in (1, 3, 2):
            middle(h, e).wait_recv()
            total = total + mid_in[h, e - 1].astype(F32)
        fgrad[:, h * H : (h + 1) * H] = total.astype(BF)

    advance(0, 1)
    w_swap.wait()
    w_sum[k] = (w_sum[k].astype(F32) + w_pair[...].astype(F32)).astype(BF)
    advance(1, 1)
    each(w_spread, begin)
    advance(0, 2)
    advance(1, 2)
    each(w_spread, landed)
    part = lax.fori_loop(
        1, NR, lambda d, total: total + w_x[d].astype(F32), w_sum[k, r].astype(F32)
    )
    w_z[z] = part.astype(BF)
    each(w_along, begin)
    advance(0, 3)
    advance(1, 3)
    advance(0, 4)
    shared(0)
    backward(0)
    advance(1, 4)
    each(w_along_in, landed)
    whole = lax.fori_loop(
        1, NZ, lambda i, total: total + w_z[i].astype(F32), w_z[0].astype(F32)
    )
    w_all[r] = whole * (1.0 / math.sqrt(NR * 2 * NZ * T))
    each(w_share, begin)
    shared(1)
    backward(1)
    back_middle(0)

    each(w_share_in, landed)
    w_far = remote(w_all, w_other, wo_send, wo_recv, partner)
    start(w_far)
    for p in range(NR):
        at = pl.multiple_of(k * 128 + (p // 2) * 16, 16)
        wgrad[pl.ds(at, 16), (p % 2) * H : (p % 2 + 1) * H] = w_all[p]
    back_middle(1)
    back_end(0)
    w_far.wait_recv()
    for p in range(NR):
        at = pl.multiple_of(other * 128 + (p // 2) * 16, 16)
        wgrad[pl.ds(at, 16), (p % 2) * H : (p % 2 + 1) * H] = w_other[p]
    for make in (w_spread, w_along, w_share):
        each(make, gone)
    back_end(1)
    for copy in sent:
        copy.wait_send()


def in_hbm(array):
    return pltpu.with_memory_space_constraint(array, pltpu.HBM)


def on_device(features, weight, tile_values, tile_rows, tile_cols, tile_count, cotangent):
    width = features.shape[1]
    dma = pltpu.SemaphoreType.DMA
    vmem = pltpu.VMEM
    hbm = pl.BlockSpec(memory_space=pltpu.HBM)
    return pl.pallas_call(
        kernel,
        out_shape=(
            jax.ShapeDtypeStruct((T, width), BF),
            jax.ShapeDtypeStruct((T, width), BF),
            jax.ShapeDtypeStruct((width, width), F32),
        ),
        in_specs=[hbm] * 5 + [pl.BlockSpec(memory_space=pltpu.SMEM), hbm],
        out_specs=(pl.BlockSpec(memory_space=pltpu.VMEM),) * 3,
        scratch_shapes=[
            vmem((width, width), BF),
            vmem((SLOTS, T, T), BF),
            vmem((1, SLOTS), jnp.int32),
            vmem((1, SLOTS), jnp.int32),
            vmem((T, width), BF),
            vmem((8, 128), jnp.int32),
            pltpu.SMEM((8, 128), jnp.int32),
            vmem((COL_T, T, H), BF),
            vmem((COL_T, T, H), BF),
            vmem((2, SLOTS + 1, T, H), F32),
            vmem((2, 4, 2, 2, T, H), BF),
            vmem((2, 4, 2, 2, T, H), BF),
            vmem((2, T, H), BF),
            vmem((2, T, H), BF),
            vmem((2, T, H), BF),
            vmem((2, 4, 2, T, H), BF),
            vmem((2, 4, 2, T, H), BF),
            vmem((2, 4, 2, T, H), BF),
            vmem((2, T, H), BF),
            vmem((2, T, H), BF),
            vmem((NZ, 2, T, H), BF),
            vmem((NZ, 2, T, H), BF),
            vmem((2, 3, NX, T, H), BF),
            vmem((2, 3, NX, T, H), BF),
            vmem((2, 3, T, H), BF),
            vmem((2, 3, T, H), BF),
            vmem((width, width), F32),
            vmem((NR, 16, 128), BF),
            vmem((2, NR, 16, 128), BF),
            vmem((NR, 16, 128), BF),
            vmem((NZ, 16, 128), BF),
            vmem((NR, 16, 128), F32),
            vmem((NR, 16, 128), F32),
            dma((7,)),
            dma,
            dma((2, 3)), dma((2, 3)),
            dma((2, 3)), dma((2, 3)),
            dma((2, 4)), dma((2, 4)),
            dma((2,)), dma((2,)),
            dma((2, 4, 2)), dma((2, 4, 2)),
            dma((2, 4)), dma((2, 4)),
            dma((2,)), dma((2,)),
            dma((2, 4, 2)), dma((2, 4, 2)),
            dma((2, 4)), dma((2, 4)),
            dma((2, 4)), dma((2, 4)),
            dma((2, 4)), dma((2, 4)),
            dma((2,)), dma((2,)),
            dma((2, 3)), dma((2, 3)),
            dma((2, 3)), dma((2, 3)),
            dma, dma,
            dma((NR,)), dma((NR,)),
            dma((NZ,)), dma((NZ,)),
            dma((NR,)), dma((NR,)),
            dma, dma,
        ],
        compiler_params=pltpu.CompilerParams(
            collective_id=0, has_side_effects=True, vmem_limit_bytes=48 * 2**20
        ),
    )(
        in_hbm(features),
        in_hbm(weight),
        in_hbm(tile_values.reshape(SLOTS, T, T)),
        in_hbm(tile_rows.reshape(1, SLOTS)),
        in_hbm(tile_cols.reshape(1, SLOTS)),
        tile_count,
        in_hbm(cotangent),
    )


def solution(mesh):
    return jax.shard_map(
        on_device,
        mesh=mesh,
        in_specs=(
            P(("col", "row"), None),
            P(),
            P("row", "col", None, None, None),
            P("row", "col", None),
            P("row", "col", None),
            P("row", "col"),
            P(("row", "col"), None),
        ),
        out_specs=(P(("row", "col"), None), P(("col", "row"), None), P()),
        check_vma=False,
    )
```

```python
import functools
import math

import jax
import jax.numpy as jnp
from jax import lax
from jax.experimental import pallas as pl
from jax.experimental.pallas import tpu as pltpu
from jax.sharding import PartitionSpec as P

MESH = pl.DeviceIdType.MESH
BF = jnp.bfloat16
F32 = jnp.float32
NX, NY, NZ, NR = 4, 4, 16, 16
SLOTS, ROW_T, COL_T, T = 32, 32, 16, 128
H = 128


def remote(src, dst, send, recv, device):
    return pltpu.make_async_remote_copy(
        src_ref=src, dst_ref=dst, send_sem=send, recv_sem=recv, device_id=device, device_id_type=MESH
    )


def slot_tables(rows, cols, count, table):
    sub = lax.broadcasted_iota(jnp.int32, (SLOTS, SLOTS), 0)
    lane = lax.broadcasted_iota(jnp.int32, (SLOTS, SLOTS), 1)
    used = sub < count

    def latest(mask):
        found = jnp.max(jnp.where(mask, sub, -1), axis=0, keepdims=True)
        return jnp.where(found < 0, SLOTS, found)

    for base, ref in ((0, rows), (2, cols)):
        along = jnp.broadcast_to(ref[...], (SLOTS, SLOTS))
        down = jnp.sum(jnp.where(sub == lane, along, 0), axis=1, keepdims=True)
        table[base : base + 1, :SLOTS] = latest((down == along) & (sub < lane) & used)
        table[base + 1 : base + 2, :SLOTS] = latest((down == lane) & used)
    table[4:5, :SLOTS] = rows[...]
    table[5:6, :SLOTS] = lax.rem(cols[...], NY) * NX + lax.div(cols[...], NY)
    table[6:7, :SLOTS] = cols[...]


def kernel(
    feat, weight_hbm, vals_hbm, rows_hbm, cols_hbm, count, cot_hbm, out, fgrad, wgrad,
    weight, vals, rows, cols, cot, table, idx, panel_a, panel_b, acc, pair_out, pair_in, own_out, own_in, first, leaf_out,
    chain_in, leaf_in, side_out, side_in, grads_a, grads_b, back_out, back_in, mid_out, mid_in,
    w_loc, w_pair, w_sum, w_x, w_z, w_all, w_other,
    in_sem, idx_sem, g_send, g_recv, gb_send, gb_recv, p_send, p_recv, o_send, o_recv, c_send, c_recv, l_send, l_recv, f_send, f_recv,
    a_send, a_recv, al_send, al_recv, q_send, q_recv, ql_send, ql_recv, t_send, t_recv, b_send, b_recv, bm_send, bm_recv,
    wp_send, wp_recv, wx_send, wx_recv, wz_send, wz_recv, wa_send, wa_recv, wo_send, wo_recv,
):
    panel, grads = (panel_a, panel_b), (grads_a, grads_b)
    r, c = lax.axis_index("row"), lax.axis_index("col")
    z, k = lax.div(c, 2), lax.rem(c, 2)
    other = 1 - k
    sigma = 1 - 2 * k
    partner = (r, 2 * z + other)

    x, y = lax.div(r, NY), lax.rem(r, NY)
    line = ((x, y), (y, x))

    def row_of(h, a, b):
        return a * NY + b if h == 0 else b * NY + a

    def along_a(h, e):
        return (row_of(h, lax.rem(line[h][0] + e, NX), line[h][1]), c)

    def along_b(h, e):
        return (row_of(h, line[h][0], lax.rem(line[h][1] + e, NX)), c)

    def at_row(d):
        return (lax.rem(r + d, NR), c)

    def at_z(d):
        return (r, 2 * lax.rem(z + d, NZ) + k)

    chips = {d: lax.rem(z + sigma * d + NZ, NZ) for d in range(-8, 9)}
    one, two = (r, 2 * chips[1] + k), (r, 2 * chips[2] + k)
    sent = []

    def start(copy):
        copy.start()
        sent.append(copy)

    def each(make, act):
        lax.fori_loop(1, NR, lambda d, u: (act(make(d)), u)[1], 0)

    def begin(copy):
        copy.start()

    def landed(copy):
        copy.wait_recv()

    def gone(copy):
        copy.wait_send()

    loads = [
        pltpu.make_async_copy(rows_hbm, rows, in_sem.at[0]),
        pltpu.make_async_copy(cols_hbm, cols, in_sem.at[1]),
        pltpu.make_async_copy(feat.at[:, 0:H], panel[0].at[y * NX + x], in_sem.at[2]),
        pltpu.make_async_copy(feat.at[:, H : 2 * H], panel[1].at[r], in_sem.at[3]),
        pltpu.make_async_copy(vals_hbm, vals, in_sem.at[4]),
        pltpu.make_async_copy(weight_hbm, weight, in_sem.at[5]),
        pltpu.make_async_copy(cot_hbm, cot, in_sem.at[6]),
    ]
    for load in loads:
        load.start()
    barrier = pltpu.get_barrier_semaphore()

    greeted = [partner]
    for e in (2, 1, 3):
        greeted += [along_a(0, e), along_b(0, e)]
    for e in (2, NZ - 2, 1, NZ - 1):
        greeted.append(at_z(e))
    for device in greeted:
        pl.semaphore_signal(barrier, inc=1, device_id=device, device_id_type=MESH)
    for h in range(2):
        acc[h, SLOTS] = jnp.zeros((T, H), F32)
    loads[0].wait()
    loads[1].wait()
    slot_tables(rows, cols, count[0, 0], table)
    to_idx = pltpu.make_async_copy(table, idx, idx_sem)
    to_idx.start()
    for load in loads[2:4]:
        load.wait()
    pl.semaphore_wait(barrier, len(greeted))

    def gather_a(h, e, a):
        tile = panel[h].at[line[h][1] * NX + a]
        return remote(tile, tile, g_send.at[h, e - 1], g_recv.at[h, e - 1], along_a(h, e))

    def gather_b(h, e, b):
        tiles = panel[h].at[pl.ds(b * NX, NX)]
        return remote(tiles, tiles, gb_send.at[h, e - 1], gb_recv.at[h, e - 1], along_b(h, e))

    for h in range(2):
        for e in (2, 1, 3):
            start(gather_a(h, e, line[h][0]))
    for h in range(2):
        for e in (1, 3, 2):
            gather_a(h, e, lax.rem(line[h][0] - e + NX, NX)).wait_recv()
        for e in (2, 1, 3):
            start(gather_b(h, e, line[h][1]))

    def forward(h):
        for e in (1, 3, 2):
            gather_b(h, e, lax.rem(line[h][1] - e + NX, NX)).wait_recv()

        def step(i, carry):
            for j in range(8):
                s = 8 * i + j
                acc[h, s] = acc[h, idx[0, s]] + jnp.dot(
                    vals[s], panel[h][idx[5 + h, s]], preferred_element_type=F32
                )
            return carry

        lax.fori_loop(0, SLOTS // 8, step, 0)

    def pair(h, g):
        return remote(pair_out.at[h, g], pair_in.at[h, g], p_send.at[h, g], p_recv.at[h, g], partner)

    def own_copy(h):
        return remote(own_out.at[h], own_in.at[h], o_send.at[h], o_recv.at[h], partner)

    def hand_over(h):
        for g in range(4):
            for j in range(2):
                for ct in range(2):
                    last = idx[1, 2 * chips[2 * g + j - 8] + ct]
                    pair_out[h, g, j, ct] = acc[h, last].astype(BF)
            start(pair(h, g))
        own_out[h] = acc[h, idx[1, 2 * z + other]].astype(BF)
        start(own_copy(h))

    def both(h, d, ct):
        last = idx[1, 2 * chips[d] + ct]
        return acc[h, last] + pair_in[h, (8 - d) // 2, (8 - d) % 2, ct].astype(F32)

    def link(h, s, ct):
        source = first.at[h] if s == 1 else chain_in.at[h, s - 2, ct]
        return remote(
            source, chain_in.at[h, s - 1, ct], c_send.at[h, s - 1, ct], c_recv.at[h, s - 1, ct], two
        )

    def leaf(h, i):
        return remote(leaf_out.at[h, i], leaf_in.at[h, i], l_send.at[h, i], l_recv.at[h, i], one)

    def send_leaf(h, i):
        for ct in range(2):
            leaf_out[h, i, ct] = both(h, 7 - 2 * i, ct).astype(BF)
        start(leaf(h, i))

    def sums_begin(h):
        pair(h, 0).wait_recv()
        first[h] = both(h, 8, k).astype(BF)
        start(link(h, 1, k))
        send_leaf(h, 0)

    def sums_step(h, s):
        pair(h, s - 1).wait_recv()
        leaf(h, s - 2).wait_recv()
        for ct in (other, k):
            total = both(h, 10 - 2 * s, ct) + leaf_in[h, s - 2, ct].astype(F32)
            if s > 2 or ct is k:
                link(h, s - 1, ct).wait_recv()
                total = total + chain_in[h, s - 2, ct].astype(F32)
            chain_in[h, s - 2, ct] = total.astype(BF)
            start(link(h, s, ct))
        send_leaf(h, s - 1)

    def side(h):
        return remote(side_out.at[h], side_in.at[h], f_send.at[h], f_recv.at[h], partner)

    def sums_end(h):
        leaf(h, 3).wait_recv()
        link(h, 4, other).wait_recv()
        side_out[h] = (chain_in[h, 3, other].astype(F32) + leaf_in[h, 3, other].astype(F32)).astype(BF)
        start(side(h))
        own_copy(h).wait_recv()
        link(h, 4, k).wait_recv()
        return (
            acc[h, idx[1, 2 * z + k]]
            + own_in[h].astype(F32)
            + chain_in[h, 3, k].astype(F32)
            + leaf_in[h, 3, k].astype(F32)
        )

    for load in loads[4:]:
        load.wait()
    to_idx.wait()
    forward(0)
    hand_over(0)
    sums_begin(0)
    forward(1)
    hand_over(1)
    sums_begin(1)
    for s in range(2, 5):
        sums_step(0, s)
        sums_step(1, s)
    halves = [sums_end(0), sums_end(1)]
    for h in range(2):
        side(h).wait_recv()
        halves[h] = (halves[h] + side_in[h].astype(F32)).astype(BF)
    aggregated = jnp.concatenate(halves, axis=1)

    preact = jnp.dot(aggregated, weight[...], preferred_element_type=F32)
    logistic = jax.nn.sigmoid(preact)
    pre_grad = (cot[...].astype(F32) * logistic * (1.0 + preact * (1.0 - logistic))).astype(BF)

    def twin(h, ct):
        tile = grads[h].at[z, ct]
        return remote(tile, tile, t_send.at[h], t_recv.at[h], partner)

    def chain(h, s, ct, at):
        tile = grads[h].at[at, ct]
        return remote(tile, tile, a_send.at[h, s - 1, ct], a_recv.at[h, s - 1, ct], two)

    def twig(h, s, at):
        tiles = grads[h].at[at]
        return remote(tiles, tiles, al_send.at[h, s - 1], al_recv.at[h, s - 1], one)

    def share(h, s, at):
        tiles = grads[h].at[at]
        return remote(tiles, tiles, q_send.at[h, s - 1], q_recv.at[h, s - 1], partner)

    def share_far(h, ct):
        tile = grads[h].at[chips[8], ct]
        return remote(tile, tile, q_send.at[h, 3], q_recv.at[h, 3], partner)

    def share_twig(h, s, at):
        tiles = grads[h].at[at]
        return remote(tiles, tiles, ql_send.at[h, s - 1], ql_recv.at[h, s - 1], partner)

    for h in range(2):
        grads[h][z, k] = lax.dot_general(
            pre_grad, weight[h * H : (h + 1) * H, :], (((1,), (1,)), ((), ())), preferred_element_type=F32
        ).astype(BF)
        start(twin(h, k))
        start(chain(h, 1, k, z))
    for h in range(2):
        twin(h, other).wait_recv()
        start(chain(h, 1, other, z))
        start(twig(h, 1, z))
    out[...] = (preact * logistic).astype(BF)
    w_loc[...] = lax.dot_general(
        aggregated, pre_grad, (((0,), (0,)), ((), ())), preferred_element_type=F32
    )
    for q in range(2):
        for p in range(NR):
            at = q * 128 + (p // 2) * 16
            w_sum[q, p] = w_loc[at : at + 16, (p % 2) * H : (p % 2 + 1) * H].astype(BF)
    w_swap = remote(w_sum.at[other], w_pair, wp_send, wp_recv, partner)
    w_swap.start()

    def advance(h, s):
        at = chips[-2 * s]
        if s < 4:
            for ct in (k, other):
                chain(h, s, ct, at).wait_recv()
                if s < 3 or ct is k:
                    start(chain(h, s + 1, ct, at))
            start(twig(h, s + 1, at))
            start(share(h, s, at))
        else:
            chain(h, 4, k, at).wait_recv()
            start(share_far(h, k))
        twig(h, s, chips[1 - 2 * s]).wait_recv()
        start(share_twig(h, s, chips[1 - 2 * s]))

    def shared(h):
        for s in range(1, 4):
            share(h, s, chips[2 * s]).wait_recv()
            share_twig(h, s, chips[2 * s - 1]).wait_recv()
        share_far(h, other).wait_recv()
        share_twig(h, 4, chips[7]).wait_recv()

    def w_spread(d):
        return remote(
            w_sum.at[k, lax.rem(r + d, NR)], w_x.at[d], wx_send.at[d], wx_recv.at[d], at_row(d)
        )

    def w_along(d):
        return remote(w_z.at[z], w_z.at[z], wz_send.at[d], wz_recv.at[d], at_z(d))

    def w_along_in(d):
        there = w_z.at[lax.rem(z - d + NZ, NZ)]
        return remote(there, there, wz_send.at[d], wz_recv.at[d], at_z(d))

    def w_share(d):
        return remote(w_all.at[r], w_all.at[r], wa_send.at[d], wa_recv.at[d], at_row(d))

    def w_share_in(d):
        there = w_all.at[lax.rem(r - d + NR, NR)]
        return remote(there, there, wa_send.at[d], wa_recv.at[d], at_row(d))

    def backward(h):
        def step(i, carry):
            for j in range(8):
                s = 8 * i + j
                row = idx[4, s]
                acc[h, s] = acc[h, idx[2, s]] + lax.dot_general(
                    vals[s],
                    grads[h][lax.div(row, 2), lax.rem(row, 2)],
                    (((0,), (0,)), ((), ())),
                    preferred_element_type=F32,
                )
            return carry

        lax.fori_loop(0, SLOTS // 8, step, 0)

        for e in (2, 1, 3):
            for a in range(NX):
                last = idx[3, row_of(h, a, lax.rem(line[h][1] + e, NX))]
                back_out[h, e - 1, a] = acc[h, last].astype(BF)
            start(back(h, e))

    def back(h, e):
        return remote(
            back_out.at[h, e - 1], back_in.at[h, e - 1], b_send.at[h, e - 1], b_recv.at[h, e - 1], along_b(h, e)
        )

    def middle(h, e):
        return remote(
            mid_out.at[h, e - 1], mid_in.at[h, e - 1], bm_send.at[h, e - 1], bm_recv.at[h, e - 1], along_a(h, e)
        )

    def line_sum(h, a):
        total = acc[h, idx[3, row_of(h, a, line[h][1])]]
        for e in range(3):
            total = total + back_in[h, e, a].astype(F32)
        return total

    def back_middle(h):
        for e in (1, 3, 2):
            back(h, e).wait_recv()
        for e in (2, 1, 3):
            mid_out[h, e - 1] = line_sum(h, lax.rem(line[h][0] + e, NX)).astype(BF)
            start(middle(h, e))

    def back_end(h):
        total = line_sum(h, line[h][0])
        for e in (1, 3, 2):
            middle(h, e).wait_recv()
            total = total + mid_in[h, e - 1].astype(F32)
        fgrad[:, h * H : (h + 1) * H] = total.astype(BF)

    advance(0, 1)
    w_swap.wait()
    w_sum[k] = (w_sum[k].astype(F32) + w_pair[...].astype(F32)).astype(BF)
    advance(1, 1)
    each(w_spread, begin)
    advance(0, 2)
    advance(1, 2)
    each(w_spread, landed)
    part = lax.fori_loop(
        1, NR, lambda d, total: total + w_x[d].astype(F32), w_sum[k, r].astype(F32)
    )
    w_z[z] = part.astype(BF)
    each(w_along, begin)
    advance(0, 3)
    advance(1, 3)
    advance(0, 4)
    shared(0)
    backward(0)
    advance(1, 4)
    each(w_along_in, landed)
    whole = lax.fori_loop(
        1, NZ, lambda i, total: total + w_z[i].astype(F32), w_z[0].astype(F32)
    )
    w_all[r] = whole * (1.0 / math.sqrt(NR * 2 * NZ * T))
    each(w_share, begin)
    shared(1)
    backward(1)
    back_middle(0)

    each(w_share_in, landed)
    w_far = remote(w_all, w_other, wo_send, wo_recv, partner)
    start(w_far)
    for p in range(NR):
        at = pl.multiple_of(k * 128 + (p // 2) * 16, 16)
        wgrad[pl.ds(at, 16), (p % 2) * H : (p % 2 + 1) * H] = w_all[p]
    back_middle(1)
    back_end(0)
    w_far.wait_recv()
    for p in range(NR):
        at = pl.multiple_of(other * 128 + (p // 2) * 16, 16)
        wgrad[pl.ds(at, 16), (p % 2) * H : (p % 2 + 1) * H] = w_other[p]
    for make in (w_spread, w_along, w_share):
        each(make, gone)
    back_end(1)
    for copy in sent:
        copy.wait_send()


def in_hbm(array):
    return pltpu.with_memory_space_constraint(array, pltpu.HBM)


def on_device(features, weight, tile_values, tile_rows, tile_cols, tile_count, cotangent):
    width = features.shape[1]
    dma = pltpu.SemaphoreType.DMA
    vmem = pltpu.VMEM
    hbm = pl.BlockSpec(memory_space=pltpu.HBM)
    return pl.pallas_call(
        kernel,
        out_shape=(
            jax.ShapeDtypeStruct((T, width), BF),
            jax.ShapeDtypeStruct((T, width), BF),
            jax.ShapeDtypeStruct((width, width), F32),
        ),
        in_specs=[hbm] * 5 + [pl.BlockSpec(memory_space=pltpu.SMEM), hbm],
        out_specs=(pl.BlockSpec(memory_space=pltpu.VMEM),) * 3,
        scratch_shapes=[
            vmem((width, width), BF),
            vmem((SLOTS, T, T), BF),
            vmem((1, SLOTS), jnp.int32),
            vmem((1, SLOTS), jnp.int32),
            vmem((T, width), BF),
            vmem((8, 128), jnp.int32),
            pltpu.SMEM((8, 128), jnp.int32),
            vmem((COL_T, T, H), BF),
            vmem((COL_T, T, H), BF),
            vmem((2, SLOTS + 1, T, H), F32),
            vmem((2, 4, 2, 2, T, H), BF),
            vmem((2, 4, 2, 2, T, H), BF),
            vmem((2, T, H), BF),
            vmem((2, T, H), BF),
            vmem((2, T, H), BF),
            vmem((2, 4, 2, T, H), BF),
            vmem((2, 4, 2, T, H), BF),
            vmem((2, 4, 2, T, H), BF),
            vmem((2, T, H), BF),
            vmem((2, T, H), BF),
            vmem((NZ, 2, T, H), BF),
            vmem((NZ, 2, T, H), BF),
            vmem((2, 3, NX, T, H), BF),
            vmem((2, 3, NX, T, H), BF),
            vmem((2, 3, T, H), BF),
            vmem((2, 3, T, H), BF),
            vmem((width, width), F32),
            vmem((NR, 16, 128), BF),
            vmem((2, NR, 16, 128), BF),
            vmem((NR, 16, 128), BF),
            vmem((NZ, 16, 128), BF),
            vmem((NR, 16, 128), F32),
            vmem((NR, 16, 128), F32),
            dma((7,)),
            dma,
            dma((2, 3)), dma((2, 3)),
            dma((2, 3)), dma((2, 3)),
            dma((2, 4)), dma((2, 4)),
            dma((2,)), dma((2,)),
            dma((2, 4, 2)), dma((2, 4, 2)),
            dma((2, 4)), dma((2, 4)),
            dma((2,)), dma((2,)),
            dma((2, 4, 2)), dma((2, 4, 2)),
            dma((2, 4)), dma((2, 4)),
            dma((2, 4)), dma((2, 4)),
            dma((2, 4)), dma((2, 4)),
            dma((2,)), dma((2,)),
            dma((2, 3)), dma((2, 3)),
            dma((2, 3)), dma((2, 3)),
            dma, dma,
            dma((NR,)), dma((NR,)),
            dma((NZ,)), dma((NZ,)),
            dma((NR,)), dma((NR,)),
            dma, dma,
        ],
        compiler_params=pltpu.CompilerParams(
            collective_id=0, has_side_effects=True, vmem_limit_bytes=48 * 2**20
        ),
    )(
        in_hbm(features),
        in_hbm(weight),
        in_hbm(tile_values.reshape(SLOTS, T, T)),
        in_hbm(tile_rows.reshape(1, SLOTS)),
        in_hbm(tile_cols.reshape(1, SLOTS)),
        tile_count,
        in_hbm(cotangent),
    )


def solution(mesh):
    return jax.shard_map(
        on_device,
        mesh=mesh,
        in_specs=(
            P(("col", "row"), None),
            P(),
            P("row", "col", None, None, None),
            P("row", "col", None),
            P("row", "col", None),
            P("row", "col"),
            P(("row", "col"), None),
        ),
        out_specs=(P(("row", "col"), None), P(("col", "row"), None), P()),
        check_vma=False,
    )
```

```python
import functools
import math

import jax
import jax.numpy as jnp
from jax import lax
from jax.experimental import pallas as pl
from jax.experimental.pallas import tpu as pltpu
from jax.sharding import PartitionSpec as P

MESH = pl.DeviceIdType.MESH
BF = jnp.bfloat16
F32 = jnp.float32
NX, NY, NZ, NR = 4, 4, 16, 16
SLOTS, ROW_T, COL_T, T = 32, 32, 16, 128
H = 128


def remote(src, dst, send, recv, device):
    return pltpu.make_async_remote_copy(
        src_ref=src, dst_ref=dst, send_sem=send, recv_sem=recv, device_id=device, device_id_type=MESH
    )


def slot_tables(rows, cols, count, table):
    sub = lax.broadcasted_iota(jnp.int32, (SLOTS, SLOTS), 0)
    lane = lax.broadcasted_iota(jnp.int32, (SLOTS, SLOTS), 1)
    used = sub < count

    def latest(mask):
        found = jnp.max(jnp.where(mask, sub, -1), axis=0, keepdims=True)
        return jnp.where(found < 0, SLOTS, found)

    for base, ref in ((0, rows), (2, cols)):
        along = jnp.broadcast_to(ref[...], (SLOTS, SLOTS))
        down = jnp.sum(jnp.where(sub == lane, along, 0), axis=1, keepdims=True)
        table[base : base + 1, :SLOTS] = latest((down == along) & (sub < lane) & used)
        table[base + 1 : base + 2, :SLOTS] = latest((down == lane) & used)
    table[4:5, :SLOTS] = rows[...]
    table[5:6, :SLOTS] = lax.rem(cols[...], NY) * NX + lax.div(cols[...], NY)
    table[6:7, :SLOTS] = cols[...]


def kernel(
    feat, weight_hbm, vals_hbm, rows_hbm, cols_hbm, count, cot_hbm, out, fgrad, wgrad,
    weight, vals, rows, cols, cot, table, idx, panel_a, panel_b, acc, pair_out, pair_in, own_out, own_in, first, leaf_out,
    chain_in, leaf_in, side_out, side_in, grads_a, grads_b, back_out, back_in, mid_out, mid_in,
    w_loc, w_pair, w_sum, w_x, w_z, w_all, w_other,
    in_sem, idx_sem, g_send, g_recv, gb_send, gb_recv, p_send, p_recv, o_send, o_recv, c_send, c_recv, l_send, l_recv, f_send, f_recv,
    a_send, a_recv, al_send, al_recv, q_send, q_recv, ql_send, ql_recv, t_send, t_recv, b_send, b_recv, bm_send, bm_recv,
    wp_send, wp_recv, wx_send, wx_recv, wz_send, wz_recv, wa_send, wa_recv, wo_send, wo_recv,
):
    panel, grads = (panel_a, panel_b), (grads_a, grads_b)
    r, c = lax.axis_index("row"), lax.axis_index("col")
    z, k = lax.div(c, 2), lax.rem(c, 2)
    other = 1 - k
    sigma = 1 - 2 * k
    partner = (r, 2 * z + other)

    x, y = lax.div(r, NY), lax.rem(r, NY)
    line = ((x, y), (y, x))

    def row_of(h, a, b):
        return a * NY + b if h == 0 else b * NY + a

    def along_a(h, e):
        return (row_of(h, lax.rem(line[h][0] + e, NX), line[h][1]), c)

    def along_b(h, e):
        return (row_of(h, line[h][0], lax.rem(line[h][1] + e, NX)), c)

    def at_row(d):
        return (lax.rem(r + d, NR), c)

    def at_z(d):
        return (r, 2 * lax.rem(z + d, NZ) + k)

    chips = {d: lax.rem(z + sigma * d + NZ, NZ) for d in range(-8, 9)}
    one, two = (r, 2 * chips[1] + k), (r, 2 * chips[2] + k)
    sent = []

    def start(copy):
        copy.start()
        sent.append(copy)

    def each(make, act):
        lax.fori_loop(1, NR, lambda d, u: (act(make(d)), u)[1], 0)

    def begin(copy):
        copy.start()

    def landed(copy):
        copy.wait_recv()

    def gone(copy):
        copy.wait_send()

    loads = [
        pltpu.make_async_copy(rows_hbm, rows, in_sem.at[0]),
        pltpu.make_async_copy(cols_hbm, cols, in_sem.at[1]),
        pltpu.make_async_copy(feat.at[:, 0:H], panel[0].at[y * NX + x], in_sem.at[2]),
        pltpu.make_async_copy(feat.at[:, H : 2 * H], panel[1].at[r], in_sem.at[3]),
        pltpu.make_async_copy(vals_hbm, vals, in_sem.at[4]),
        pltpu.make_async_copy(weight_hbm, weight, in_sem.at[5]),
        pltpu.make_async_copy(cot_hbm, cot, in_sem.at[6]),
    ]
    for load in loads:
        load.start()
    barrier = pltpu.get_barrier_semaphore()

    greeted = [partner]
    for e in (2, 1, 3):
        greeted += [along_a(0, e), along_b(0, e)]
    for e in (2, NZ - 2, 1, NZ - 1):
        greeted.append(at_z(e))
    for device in greeted:
        pl.semaphore_signal(barrier, inc=1, device_id=device, device_id_type=MESH)
    for h in range(2):
        acc[h, SLOTS] = jnp.zeros((T, H), F32)
    loads[0].wait()
    loads[1].wait()
    slot_tables(rows, cols, count[0, 0], table)
    to_idx = pltpu.make_async_copy(table, idx, idx_sem)
    to_idx.start()
    for load in loads[2:4]:
        load.wait()
    pl.semaphore_wait(barrier, len(greeted))

    def gather_a(h, e, a):
        tile = panel[h].at[line[h][1] * NX + a]
        return remote(tile, tile, g_send.at[h, e - 1], g_recv.at[h, e - 1], along_a(h, e))

    def gather_b(h, e, b):
        tiles = panel[h].at[pl.ds(b * NX, NX)]
        return remote(tiles, tiles, gb_send.at[h, e - 1], gb_recv.at[h, e - 1], along_b(h, e))

    for h in range(2):
        for e in (2, 1, 3):
            start(gather_a(h, e, line[h][0]))
    for h in range(2):
        for e in (1, 3, 2):
            gather_a(h, e, lax.rem(line[h][0] - e + NX, NX)).wait_recv()
        for e in (2, 1, 3):
            start(gather_b(h, e, line[h][1]))

    def forward(h):
        for e in (1, 3, 2):
            gather_b(h, e, lax.rem(line[h][1] - e + NX, NX)).wait_recv()

        def step(i, carry):
            for j in range(8):
                s = 8 * i + j
                acc[h, s] = acc[h, idx[0, s]] + jnp.dot(
                    vals[s], panel[h][idx[5 + h, s]], preferred_element_type=F32
                )
            return carry

        lax.fori_loop(0, SLOTS // 8, step, 0)

    def pair(h, g):
        return remote(pair_out.at[h, g], pair_in.at[h, g], p_send.at[h, g], p_recv.at[h, g], partner)

    def own_copy(h):
        return remote(own_out.at[h], own_in.at[h], o_send.at[h], o_recv.at[h], partner)

    def hand_over(h):
        for g in range(4):
            for j in range(2):
                for ct in range(2):
                    last = idx[1, 2 * chips[2 * g + j - 8] + ct]
                    pair_out[h, g, j, ct] = acc[h, last].astype(BF)
            start(pair(h, g))
        own_out[h] = acc[h, idx[1, 2 * z + other]].astype(BF)
        start(own_copy(h))

    def both(h, d, ct):
        last = idx[1, 2 * chips[d] + ct]
        return acc[h, last] + pair_in[h, (8 - d) // 2, (8 - d) % 2, ct].astype(F32)

    def link(h, s, ct):
        source = first.at[h] if s == 1 else chain_in.at[h, s - 2, ct]
        return remote(
            source, chain_in.at[h, s - 1, ct], c_send.at[h, s - 1, ct], c_recv.at[h, s - 1, ct], two
        )

    def leaf(h, i):
        return remote(leaf_out.at[h, i], leaf_in.at[h, i], l_send.at[h, i], l_recv.at[h, i], one)

    def send_leaf(h, i):
        for ct in range(2):
            leaf_out[h, i, ct] = both(h, 7 - 2 * i, ct).astype(BF)
        start(leaf(h, i))

    def sums_begin(h):
        pair(h, 0).wait_recv()
        first[h] = both(h, 8, k).astype(BF)
        start(link(h, 1, k))
        send_leaf(h, 0)

    def sums_step(h, s):
        leaf(h, s - 2).wait_recv()
        for ct in (other, k):
            total = both(h, 10 - 2 * s, ct) + leaf_in[h, s - 2, ct].astype(F32)
            if s > 2 or ct is k:
                link(h, s - 1, ct).wait_recv()
                total = total + chain_in[h, s - 2, ct].astype(F32)
            chain_in[h, s - 2, ct] = total.astype(BF)
            start(link(h, s, ct))

    def side(h):
        return remote(side_out.at[h], side_in.at[h], f_send.at[h], f_recv.at[h], partner)

    def sums_end(h):
        leaf(h, 3).wait_recv()
        link(h, 4, other).wait_recv()
        side_out[h] = (chain_in[h, 3, other].astype(F32) + leaf_in[h, 3, other].astype(F32)).astype(BF)
        start(side(h))
        own_copy(h).wait_recv()
        link(h, 4, k).wait_recv()
        return (
            acc[h, idx[1, 2 * z + k]]
            + own_in[h].astype(F32)
            + chain_in[h, 3, k].astype(F32)
            + leaf_in[h, 3, k].astype(F32)
        )

    for load in loads[4:]:
        load.wait()
    to_idx.wait()
    forward(0)
    hand_over(0)
    sums_begin(0)
    forward(1)
    hand_over(1)
    sums_begin(1)
    for s in range(2, 5):
        for h in range(2):
            pair(h, s - 1).wait_recv()
            send_leaf(h, s - 1)
        sums_step(0, s)
        sums_step(1, s)
    halves = [sums_end(0), sums_end(1)]
    for h in range(2):
        side(h).wait_recv()
        halves[h] = (halves[h] + side_in[h].astype(F32)).astype(BF)
    aggregated = jnp.concatenate(halves, axis=1)

    preact = jnp.dot(aggregated, weight[...], preferred_element_type=F32)
    logistic = jax.nn.sigmoid(preact)
    pre_grad = (cot[...].astype(F32) * logistic * (1.0 + preact * (1.0 - logistic))).astype(BF)

    def twin(h, ct):
        tile = grads[h].at[z, ct]
        return remote(tile, tile, t_send.at[h], t_recv.at[h], partner)

    def chain(h, s, ct, at):
        tile = grads[h].at[at, ct]
        return remote(tile, tile, a_send.at[h, s - 1, ct], a_recv.at[h, s - 1, ct], two)

    def twig(h, s, at):
        tiles = grads[h].at[at]
        return remote(tiles, tiles, al_send.at[h, s - 1], al_recv.at[h, s - 1], one)

    def share(h, s, at):
        tiles = grads[h].at[at]
        return remote(tiles, tiles, q_send.at[h, s - 1], q_recv.at[h, s - 1], partner)

    def share_far(h, ct):
        tile = grads[h].at[chips[8], ct]
        return remote(tile, tile, q_send.at[h, 3], q_recv.at[h, 3], partner)

    def share_twig(h, s, at):
        tiles = grads[h].at[at]
        return remote(tiles, tiles, ql_send.at[h, s - 1], ql_recv.at[h, s - 1], partner)

    for h in range(2):
        grads[h][z, k] = lax.dot_general(
            pre_grad, weight[h * H : (h + 1) * H, :], (((1,), (1,)), ((), ())), preferred_element_type=F32
        ).astype(BF)
        start(twin(h, k))
        start(chain(h, 1, k, z))
    for h in range(2):
        twin(h, other).wait_recv()
        start(chain(h, 1, other, z))
        start(twig(h, 1, z))
    out[...] = (preact * logistic).astype(BF)
    w_loc[...] = lax.dot_general(
        aggregated, pre_grad, (((0,), (0,)), ((), ())), preferred_element_type=F32
    )
    for q in range(2):
        for p in range(NR):
            at = q * 128 + (p // 2) * 16
            w_sum[q, p] = w_loc[at : at + 16, (p % 2) * H : (p % 2 + 1) * H].astype(BF)
    w_swap = remote(w_sum.at[other], w_pair, wp_send, wp_recv, partner)
    w_swap.start()

    def advance(h, s):
        at = chips[-2 * s]
        if s < 4:
            for ct in (k, other):
                chain(h, s, ct, at).wait_recv()
                if s < 3 or ct is k:
                    start(chain(h, s + 1, ct, at))
            start(twig(h, s + 1, at))
            start(share(h, s, at))
        else:
            chain(h, 4, k, at).wait_recv()
            start(share_far(h, k))
        twig(h, s, chips[1 - 2 * s]).wait_recv()
        start(share_twig(h, s, chips[1 - 2 * s]))

    def shared(h):
        for s in range(1, 4):
            share(h, s, chips[2 * s]).wait_recv()
            share_twig(h, s, chips[2 * s - 1]).wait_recv()
        share_far(h, other).wait_recv()
        share_twig(h, 4, chips[7]).wait_recv()

    def w_spread(d):
        return remote(
            w_sum.at[k, lax.rem(r + d, NR)], w_x.at[d], wx_send.at[d], wx_recv.at[d], at_row(d)
        )

    def w_along(d):
        return remote(w_z.at[z], w_z.at[z], wz_send.at[d], wz_recv.at[d], at_z(d))

    def w_along_in(d):
        there = w_z.at[lax.rem(z - d + NZ, NZ)]
        return remote(there, there, wz_send.at[d], wz_recv.at[d], at_z(d))

    def w_share(d):
        return remote(w_all.at[r], w_all.at[r], wa_send.at[d], wa_recv.at[d], at_row(d))

    def w_share_in(d):
        there = w_all.at[lax.rem(r - d + NR, NR)]
        return remote(there, there, wa_send.at[d], wa_recv.at[d], at_row(d))

    def backward(h):
        def step(i, carry):
            for j in range(8):
                s = 8 * i + j
                row = idx[4, s]
                acc[h, s] = acc[h, idx[2, s]] + lax.dot_general(
                    vals[s],
                    grads[h][lax.div(row, 2), lax.rem(row, 2)],
                    (((0,), (0,)), ((), ())),
                    preferred_element_type=F32,
                )
            return carry

        lax.fori_loop(0, SLOTS // 8, step, 0)

        for e in (2, 1, 3):
            for a in range(NX):
                last = idx[3, row_of(h, a, lax.rem(line[h][1] + e, NX))]
                back_out[h, e - 1, a] = acc[h, last].astype(BF)
            start(back(h, e))

    def back(h, e):
        return remote(
            back_out.at[h, e - 1], back_in.at[h, e - 1], b_send.at[h, e - 1], b_recv.at[h, e - 1], along_b(h, e)
        )

    def middle(h, e):
        return remote(
            mid_out.at[h, e - 1], mid_in.at[h, e - 1], bm_send.at[h, e - 1], bm_recv.at[h, e - 1], along_a(h, e)
        )

    def line_sum(h, a):
        total = acc[h, idx[3, row_of(h, a, line[h][1])]]
        for e in range(3):
            total = total + back_in[h, e, a].astype(F32)
        return total

    def back_middle(h):
        for e in (1, 3, 2):
            back(h, e).wait_recv()
        for e in (2, 1, 3):
            mid_out[h, e - 1] = line_sum(h, lax.rem(line[h][0] + e, NX)).astype(BF)
            start(middle(h, e))

    def back_end(h):
        total = line_sum(h, line[h][0])
        for e in (1, 3, 2):
            middle(h, e).wait_recv()
            total = total + mid_in[h, e - 1].astype(F32)
        fgrad[:, h * H : (h + 1) * H] = total.astype(BF)

    advance(0, 1)
    w_swap.wait()
    w_sum[k] = (w_sum[k].astype(F32) + w_pair[...].astype(F32)).astype(BF)
    advance(1, 1)
    each(w_spread, begin)
    advance(0, 2)
    advance(1, 2)
    each(w_spread, landed)
    part = lax.fori_loop(
        1, NR, lambda d, total: total + w_x[d].astype(F32), w_sum[k, r].astype(F32)
    )
    w_z[z] = part.astype(BF)
    each(w_along, begin)
    advance(0, 3)
    advance(1, 3)
    advance(0, 4)
    shared(0)
    backward(0)
    advance(1, 4)
    each(w_along_in, landed)
    whole = lax.fori_loop(
        1, NZ, lambda i, total: total + w_z[i].astype(F32), w_z[0].astype(F32)
    )
    w_all[r] = whole * (1.0 / math.sqrt(NR * 2 * NZ * T))
    each(w_share, begin)
    shared(1)
    backward(1)
    back_middle(0)

    each(w_share_in, landed)
    w_far = remote(w_all, w_other, wo_send, wo_recv, partner)
    start(w_far)
    for p in range(NR):
        at = pl.multiple_of(k * 128 + (p // 2) * 16, 16)
        wgrad[pl.ds(at, 16), (p % 2) * H : (p % 2 + 1) * H] = w_all[p]
    back_middle(1)
    back_end(0)
    w_far.wait_recv()
    for p in range(NR):
        at = pl.multiple_of(other * 128 + (p // 2) * 16, 16)
        wgrad[pl.ds(at, 16), (p % 2) * H : (p % 2 + 1) * H] = w_other[p]
    for make in (w_spread, w_along, w_share):
        each(make, gone)
    back_end(1)
    for copy in sent:
        copy.wait_send()


def in_hbm(array):
    return pltpu.with_memory_space_constraint(array, pltpu.HBM)


def on_device(features, weight, tile_values, tile_rows, tile_cols, tile_count, cotangent):
    width = features.shape[1]
    dma = pltpu.SemaphoreType.DMA
    vmem = pltpu.VMEM
    hbm = pl.BlockSpec(memory_space=pltpu.HBM)
    return pl.pallas_call(
        kernel,
        out_shape=(
            jax.ShapeDtypeStruct((T, width), BF),
            jax.ShapeDtypeStruct((T, width), BF),
            jax.ShapeDtypeStruct((width, width), F32),
        ),
        in_specs=[hbm] * 5 + [pl.BlockSpec(memory_space=pltpu.SMEM), hbm],
        out_specs=(pl.BlockSpec(memory_space=pltpu.VMEM),) * 3,
        scratch_shapes=[
            vmem((width, width), BF),
            vmem((SLOTS, T, T), BF),
            vmem((1, SLOTS), jnp.int32),
            vmem((1, SLOTS), jnp.int32),
            vmem((T, width), BF),
            vmem((8, 128), jnp.int32),
            pltpu.SMEM((8, 128), jnp.int32),
            vmem((COL_T, T, H), BF),
            vmem((COL_T, T, H), BF),
            vmem((2, SLOTS + 1, T, H), F32),
            vmem((2, 4, 2, 2, T, H), BF),
            vmem((2, 4, 2, 2, T, H), BF),
            vmem((2, T, H), BF),
            vmem((2, T, H), BF),
            vmem((2, T, H), BF),
            vmem((2, 4, 2, T, H), BF),
            vmem((2, 4, 2, T, H), BF),
            vmem((2, 4, 2, T, H), BF),
            vmem((2, T, H), BF),
            vmem((2, T, H), BF),
            vmem((NZ, 2, T, H), BF),
            vmem((NZ, 2, T, H), BF),
            vmem((2, 3, NX, T, H), BF),
            vmem((2, 3, NX, T, H), BF),
            vmem((2, 3, T, H), BF),
            vmem((2, 3, T, H), BF),
            vmem((width, width), F32),
            vmem((NR, 16, 128), BF),
            vmem((2, NR, 16, 128), BF),
            vmem((NR, 16, 128), BF),
            vmem((NZ, 16, 128), BF),
            vmem((NR, 16, 128), F32),
            vmem((NR, 16, 128), F32),
            dma((7,)),
            dma,
            dma((2, 3)), dma((2, 3)),
            dma((2, 3)), dma((2, 3)),
            dma((2, 4)), dma((2, 4)),
            dma((2,)), dma((2,)),
            dma((2, 4, 2)), dma((2, 4, 2)),
            dma((2, 4)), dma((2, 4)),
            dma((2,)), dma((2,)),
            dma((2, 4, 2)), dma((2, 4, 2)),
            dma((2, 4)), dma((2, 4)),
            dma((2, 4)), dma((2, 4)),
            dma((2, 4)), dma((2, 4)),
            dma((2,)), dma((2,)),
            dma((2, 3)), dma((2, 3)),
            dma((2, 3)), dma((2, 3)),
            dma, dma,
            dma((NR,)), dma((NR,)),
            dma((NZ,)), dma((NZ,)),
            dma((NR,)), dma((NR,)),
            dma, dma,
        ],
        compiler_params=pltpu.CompilerParams(
            collective_id=0, has_side_effects=True, vmem_limit_bytes=48 * 2**20
        ),
    )(
        in_hbm(features),
        in_hbm(weight),
        in_hbm(tile_values.reshape(SLOTS, T, T)),
        in_hbm(tile_rows.reshape(1, SLOTS)),
        in_hbm(tile_cols.reshape(1, SLOTS)),
        tile_count,
        in_hbm(cotangent),
    )


def solution(mesh):
    return jax.shard_map(
        on_device,
        mesh=mesh,
        in_specs=(
            P(("col", "row"), None),
            P(),
            P("row", "col", None, None, None),
            P("row", "col", None),
            P("row", "col", None),
            P("row", "col"),
            P(("row", "col"), None),
        ),
        out_specs=(P(("row", "col"), None), P(("col", "row"), None), P()),
        check_vma=False,
    )
```
